128 devices in a mesh: dp: 32 (over z, y, core), segment: 4 (over x).
Axes of the slice: x: 4, y: 4, z: 4, core: 2. Of those that a mesh axis runs over, the one named last changes fastest.
Arguments:
- patches: bfloat16 [4, 512, 64, 588], P('segment', 'dp'), may hold values from -6 to 6
- image_shape: int32 [4, 512, 2], P('segment', 'dp'), may hold values from 6 to 8
- keep_list: int32 [4, 512, 32], P('segment', 'dp'), may hold values from 0 to 63, as said below
- kept_count: int32 [4, 512], P('segment', 'dp'), may hold values from 16 to 32
- dest_seq: int32 [4, 512], P('segment', 'dp'), may hold values from 0 to 31, as said below
- embed_weight: bfloat16 [588, 6144], replicated, may hold values from -0.25 to 0.25
- pos_rows: bfloat16 [8, 6144], replicated, may hold values from -3 to 3
- pos_cols: bfloat16 [8, 6144], replicated, may hold values from -3 to 3
- ln_gain: bfloat16 [4, 6144], P('segment'), may hold values from 0.099609375 to 1.8984375
- qkv_weight: bfloat16 [4, 6144, 384], P('segment'), may hold values from -10 to 10
- norm_gains: float32 [4, 2, 128], P('segment'), may hold values from 0.5 to 4
- out_weight: bfloat16 [4, 128, 6144], P('segment'), may hold values from -0.5 to 0.5
Outputs:
- handed: bfloat16 [4, 16384, 6144], P('segment', 'dp')
The draws below stay inside these ranges and needn't reach their ends.
Inputs may be any that keep to these rules, and one draw needn't show every extreme that they name: `dest_seq`: each device's 16 images go to 16 sequences' worth of slots: every sequence receives exactly 16 images, at most 1 from one device; the kept patches from one device to one sequence number at most 32 and those of one sequence at most 512, both reached in every micro-batch. `keep_list`: entries of one image are distinct and below its height times width.
All inputs are finite; a program needn't handle non-finite values.
Results may differ from the reference program's by a relative error of at most 0.023.
The reference program's roundings to bfloat16 on the way count: a program that leaves them out, or rounds other values in their place, can miss the bound.
Values may be sent and summed in bfloat16 or wider, within the bound.
No kernel may reach another device: no remote copies, remote signals or barrier semaphores. Data moves between devices by JAX's collectives and lax.ppermute only.
A program may use at most 128 MiB of HBM per device.

```python
import math
import jax
import jax.numpy as jnp
from jax import lax

D = 6144
HEAD_DIM = 128
PATCH_DIM = 588
HEADS_WIN = 1
SEQ_LEN = 512
KEPT_MAX = 32
SIDE_MAX = 8
PATCH_MAX = 64
IMG_SEQ = 16
IMAGES = 512
SEQ_ALL = 16384
N_DP = 32
N_SEGMENT = 4


def layout(key):
    segments = N_SEGMENT
    groups = N_DP
    per_dev = IMG_SEQ
    keys = jax.random.split(key, 6)
    shifts = jax.vmap(lambda one: jax.random.permutation(one, groups))(jax.random.split(keys[0], segments))
    offsets = shifts[:, jnp.arange(per_dev) % groups]
    shuffles = jax.vmap(lambda one: jax.random.permutation(one, per_dev))(jax.random.split(keys[1], segments * groups))
    shuffles = shuffles.reshape(segments, groups, per_dev)
    chosen = jnp.take_along_axis(jnp.broadcast_to(offsets[:, None, :], (segments, groups, per_dev)), shuffles, axis=2)
    source = jnp.arange(groups, dtype=jnp.int32)[None, :, None]
    dest = ((source + chosen) % groups).reshape(segments, IMAGES).astype(jnp.int32)
    full_seq = jax.random.randint(keys[2], (segments, 1), 0, groups)
    counts = jax.random.randint(keys[3], (segments, IMAGES), KEPT_MAX // 2, KEPT_MAX + 1)
    counts = jnp.where(dest == full_seq, KEPT_MAX, counts).astype(jnp.int32)
    shape_hw = jax.random.randint(keys[4], (segments, IMAGES, 2), 6, SIDE_MAX + 1).astype(jnp.int32)
    ranks = jax.vmap(lambda one: jax.random.permutation(one, PATCH_MAX))(jax.random.split(keys[5], segments * IMAGES))
    area = (shape_hw[..., 0] * shape_hw[..., 1]).reshape(-1)
    slots = jnp.arange(PATCH_MAX, dtype=jnp.int32)
    scores = ranks + jnp.where(slots[None, :] >= area[:, None], PATCH_MAX, 0)
    picks = jnp.argsort(scores, axis=1, stable=True)[:, :KEPT_MAX]
    return (dest, counts, shape_hw, picks.reshape(segments, IMAGES, KEPT_MAX).astype(jnp.int32))


def draw_image_shape(key, part):
    return layout(key)[2]


def draw_keep_list(key, part):
    return layout(key)[3]


def draw_kept_count(key, part):
    return layout(key)[1]


def draw_dest_seq(key, part):
    return layout(key)[0]


def draw_qkv_weight(key, part):
    key = jax.random.fold_in(key, 7)
    keys = jax.random.split(key, 1)
    width = HEADS_WIN * HEAD_DIM
    shape = (N_SEGMENT, D, 3 * width)
    scale = 1.0 / math.sqrt(D)
    base = jnp.clip(jax.random.normal(keys[0], shape, jnp.float32), -6.0, 6.0) * scale
    return base.astype(jnp.bfloat16)


def draw_norm_gains(key, part):
    key = jax.random.fold_in(key, 9)
    shape = (N_SEGMENT, 2, HEAD_DIM)
    return jnp.exp(jax.random.uniform(key, shape, jnp.float32, math.log(0.5), math.log(4.0)))


def level_of(own_key, dims, cuts, least, largest):
    loudness, own = 1.0, jax.random.fold_in(own_key, 6)
    for position, parts in cuts:
        draws = jnp.exp(jax.random.uniform(jax.random.fold_in(own, position), (parts,), jnp.float32, least / len(cuts), largest / len(cuts)))
        loudness = loudness * jnp.repeat(draws, dims[position] // parts).reshape([-1 if axis == position else 1 for axis in range(len(dims))])
    return loudness


def scatter_about(own_key, dims, scale, bound, shards=(), kind=jnp.bfloat16):
    level = level_of(own_key, dims, shards, -0.22, 0.18) if shards else 1.0
    values = jax.random.normal(own_key, dims, jnp.float32) * scale * level
    return jnp.minimum(jnp.maximum(values, -bound), bound).astype(kind)


def setup_inputs(seed: int = 0) -> dict:
    streams_of = jax.random.split(jax.random.key(seed), 13)
    return {
        "patches": scatter_about(streams_of[0], (N_SEGMENT, IMAGES, PATCH_MAX, PATCH_DIM), 1.0, 6.0, ((0, 4), (1, 32))),
        "image_shape": draw_image_shape(jax.random.fold_in(streams_of[12], 71), 0),
        "keep_list": draw_keep_list(jax.random.fold_in(streams_of[12], 71), 0),
        "kept_count": draw_kept_count(jax.random.fold_in(streams_of[12], 71), 0),
        "dest_seq": draw_dest_seq(jax.random.fold_in(streams_of[12], 71), 0),
        "embed_weight": scatter_about(streams_of[5], (PATCH_DIM, D), PATCH_DIM ** -0.5, 0.25),
        "pos_rows": scatter_about(streams_of[6], (SIDE_MAX, D), 0.5, 3.0),
        "pos_cols": scatter_about(streams_of[7], (SIDE_MAX, D), 0.5, 3.0),
        "ln_gain": jnp.clip(1.0 + 0.18 * jax.random.normal(streams_of[8], (N_SEGMENT, D), jnp.float32), 0.099609375, 1.8984375).astype(jnp.bfloat16),
        "qkv_weight": draw_qkv_weight(jax.random.fold_in(streams_of[12], 71), 0),
        "norm_gains": draw_norm_gains(jax.random.fold_in(streams_of[12], 71), 0),
        "out_weight": scatter_about(streams_of[11], (N_SEGMENT, HEADS_WIN * HEAD_DIM, D), (HEADS_WIN * HEAD_DIM) ** -0.5, 0.5, ((0, 4),)),
    }


eps = 1e-06

def embed_rows(raw_rows, row_index, col_index, embed_weight, pos_rows, pos_cols):
    levels = jnp.arange(pos_rows.shape[0], dtype=jnp.int32)
    row_hot = (row_index[:, None] == levels[None, :]).astype(jnp.bfloat16)
    col_hot = (col_index[:, None] == levels[None, :]).astype(jnp.bfloat16)
    total = jnp.dot(raw_rows, embed_weight, preferred_element_type=jnp.float32)
    total = total + jnp.dot(row_hot, pos_rows, preferred_element_type=jnp.float32)
    return total + jnp.dot(col_hot, pos_cols, preferred_element_type=jnp.float32)

def head_norm(values, gain):
    centre = values - lax.optimization_barrier(jnp.mean(values, axis=-1, keepdims=True))
    spread = lax.optimization_barrier(jnp.mean(centre * centre, axis=-1, keepdims=True))
    return (centre * lax.rsqrt(spread + eps) * gain).astype(jnp.bfloat16)

def section_layer(tokens, seq_ids, ln_gain, qkv_weight, norm_gains, out_weight):
    seq_len = tokens.shape[0]
    head_dim = norm_gains.shape[1]
    width = out_weight.shape[0]
    heads = width // head_dim
    floats = tokens.astype(jnp.float32)
    centre = floats - lax.optimization_barrier(jnp.mean(floats, axis=1, keepdims=True))
    spread = lax.optimization_barrier(jnp.mean(centre * centre, axis=1, keepdims=True))
    normed = (centre * lax.rsqrt(spread + eps) * ln_gain.astype(jnp.float32)).astype(jnp.bfloat16)
    mixed = jnp.dot(normed, qkv_weight, preferred_element_type=jnp.float32)
    queries = head_norm(mixed[:, :width].reshape(seq_len, heads, head_dim), norm_gains[0])
    keys = head_norm(mixed[:, width:2 * width].reshape(seq_len, heads, head_dim), norm_gains[1])
    values = mixed[:, 2 * width:].reshape(seq_len, heads, head_dim).astype(jnp.bfloat16)
    scores = jnp.einsum('qhd,khd->hqk', queries.astype(jnp.float32), keys.astype(jnp.float32)) / math.sqrt(head_dim)
    allowed = seq_ids[:, None] == seq_ids[None, :]
    scores = jnp.where(allowed[None], scores, -jnp.inf)
    top = lax.optimization_barrier(jnp.max(scores, axis=-1, keepdims=True))
    expo = jnp.exp(scores - top)
    weights = (expo / lax.optimization_barrier(jnp.sum(expo, axis=-1, keepdims=True))).astype(jnp.bfloat16)
    attended = jnp.einsum('hqk,khd->qhd', weights.astype(jnp.float32), values.astype(jnp.float32))
    attended = attended.astype(jnp.bfloat16).reshape(seq_len, width)
    result = floats + jnp.dot(attended, out_weight, preferred_element_type=jnp.float32)
    return jnp.where((seq_ids >= 0)[:, None], result, 0.0).astype(jnp.bfloat16)

def reference(patches, image_shape, keep_list, kept_count, dest_seq, embed_weight, pos_rows, pos_cols, ln_gain, qkv_weight, norm_gains, out_weight):
    results = []
    for segment_idx in range(N_SEGMENT):
        counts = kept_count[segment_idx]
        targets = dest_seq[segment_idx]
        order = jnp.arange(IMAGES, dtype=jnp.int32)
        earlier = (order[None, :] < order[:, None]) & (targets[None, :] == targets[:, None])
        within = lax.optimization_barrier(jnp.sum(jnp.where(earlier, counts[None, :], 0), axis=1)).astype(jnp.int32)
        picks = keep_list[segment_idx]
        widths = image_shape[segment_idx][:, 1]
        row_index = (picks // widths[:, None]).astype(jnp.int32)
        col_index = (picks % widths[:, None]).astype(jnp.int32)
        raw = jnp.take_along_axis(patches[segment_idx], picks[:, :, None], axis=1)
        embedded = embed_rows(raw.reshape(-1, PATCH_DIM), row_index.reshape(-1), col_index.reshape(-1), embed_weight, pos_rows, pos_cols).astype(jnp.bfloat16)
        offsets = jnp.arange(KEPT_MAX, dtype=jnp.int32)
        live = offsets[None, :] < counts[:, None]
        place = jnp.where(live, targets[:, None] * SEQ_LEN + within[:, None] + offsets[None, :], SEQ_ALL).astype(jnp.int32).reshape(-1)
        tokens = jnp.zeros((SEQ_ALL, D), jnp.bfloat16).at[place].set(embedded, mode='drop')
        image_ids = jnp.broadcast_to(order[:, None], (IMAGES, KEPT_MAX)).reshape(-1)
        seq_ids = jnp.full((SEQ_ALL,), -1, jnp.int32).at[place].set(image_ids, mode='drop')

        def run_one(pair):
            return section_layer(pair[0], pair[1], ln_gain[segment_idx], qkv_weight[segment_idx], norm_gains[segment_idx], out_weight[segment_idx])
        outputs = lax.map(run_one, (tokens.reshape(N_DP, SEQ_LEN, D), seq_ids.reshape(N_DP, SEQ_LEN)))
        results.append(outputs.reshape(SEQ_ALL, D))
    return jnp.roll(jnp.stack(results), 1, axis=0)
```

```python
import math

import jax
import jax.numpy as jnp
from jax import lax
from jax.experimental import pallas as pl
from jax.experimental.pallas import tpu as pltpu
from jax.sharding import PartitionSpec as P

eps = 1e-06
LANES = 640
TAIL = 512
ROW_AT = 588 - TAIL
COL_AT = 596 - TAIL
SRC_AT = 604 - TAIL
SRC_END = 636 - TAIL
TILE = 1024
EARLY = 2
STORE = 20480
MIB = 1 << 20


def iota(shape, axis):
    return lax.broadcasted_iota(jnp.int32, shape, axis)


def dot(a, b, dims=((1,), (0,))):
    return lax.dot_general(a, b, (dims, ((), ())), preferred_element_type=jnp.float32)


def as_bf16(mask):
    return mask.astype(jnp.float32).astype(jnp.bfloat16)


def pack_kernel(
    shape_hbm, count_hbm, dest_hbm, keep_hbm, patches_hbm, weight_hbm, out_ref, half_ref, token_ref,
    shape, count, dest, keep, patches, sems, patch_sems,
):
    images, patch_max, _ = patches.shape
    kept_max = keep.shape[1]
    parts = patch_sems.shape[0]
    step = images // parts
    small = [
        pltpu.make_async_copy(source, target, sems.at[n])
        for n, (source, target) in enumerate(
            ((shape_hbm, shape), (count_hbm, count), (dest_hbm, dest), (keep_hbm, keep))
        )
    ]
    large = [
        pltpu.make_async_copy(
            patches_hbm.at[pl.ds(n * step, step)], patches.at[pl.ds(n * step, step)], patch_sems.at[n]
        )
        for n in range(parts)
    ]
    for copy in small + large:
        copy.start()
    device = lax.axis_index("dp")
    share = half_ref.shape[0]
    half = pltpu.make_async_copy(
        weight_hbm.at[pl.ds(pl.multiple_of(device % 2 * share, share), share)], half_ref, sems.at[4]
    )
    half.start()
    out_ref[...] = jnp.zeros_like(out_ref)
    token_ref[...] = jnp.zeros_like(token_ref)
    number = iota((patch_max, 128), 0)
    lane = iota((patch_max, 128), 1)
    source = lane == SRC_AT + device
    for copy in small:
        copy.wait()
    for g in range(images):
        if g % step == 0:
            large[g // step].wait()
        width = shape[1, g]
        row = jnp.zeros_like(number)
        for k in range(1, 8):
            row = row + (number >= k * width).astype(jnp.int32)
        col = number - row * width
        flags = as_bf16((lane == ROW_AT + row) | (lane == COL_AT + col) | source)
        picked = (iota((patch_max, kept_max), 0) == keep[g : g + 1, :]) & (
            iota((patch_max, kept_max), 1) < count[0, g]
        )
        picked = as_bf16(picked)
        there = dest[0, g]
        body = dot(picked, patches[g, :, :TAIL], ((0,), (0,)))
        out_ref[there, :, :TAIL] = body.astype(jnp.bfloat16)
        last = jnp.concatenate([patches[g, :, TAIL:], flags[:, ROW_AT:]], axis=1)
        out_ref[there, :, TAIL:] = dot(picked, last, ((0,), (0,))).astype(jnp.bfloat16)
    half.wait()


def compact_kernel(weights_hbm, recv_ref, out_ref, early_ref, sems):
    copies = tile_copies(weights_hbm, 0, early_ref, sems)
    for copy in copies:
        copy.start()
    sources, kept_max, lanes = recv_ref.shape
    total = sources * kept_max
    blocks = total // 128
    seq_len = out_ref.shape[0]
    received = recv_ref[...].reshape(total, lanes)
    at = iota((8, 128), 1)
    select = as_bf16((at >= SRC_AT) & (at < SRC_END))
    live = dot(select, received[:, TAIL:], ((1,), (1,)))
    group = iota((8, 128), 0)
    packed = jnp.zeros((8, 128), jnp.float32)
    for b in range(blocks):
        packed = jnp.where(group == b, live[:, b * 128 : (b + 1) * 128], packed)
    before = as_bf16(iota((128, 128), 0) < iota((128, 128), 1))
    within = dot(packed.astype(jnp.bfloat16), before)
    sums = jnp.sum(packed, axis=1, keepdims=True)
    base = jnp.zeros((8, 1), jnp.float32)
    for b in range(blocks - 1):
        base = base + jnp.where(iota((8, 1), 0) > b, sums[b : b + 1, :], 0.0)
    place = jnp.where(packed > 0.5, within + base, -1.0).astype(jnp.int32)
    slot = iota((seq_len, 128), 0)
    hot = jnp.concatenate([as_bf16(slot == place[b : b + 1, :]) for b in range(blocks)], axis=1)
    out_ref[...] = dot(hot, received).astype(jnp.bfloat16)
    for copy in copies:
        copy.wait()


def lane_sums(values, sums):
    for at in range(0, values.shape[1], 128):
        sums = sums + values[:, at : at + 128]
    return sums


def head_norm(values, gain):
    centre = values - jnp.mean(values, axis=-1, keepdims=True)
    spread = jnp.mean(centre * centre, axis=-1, keepdims=True)
    return (centre * lax.rsqrt(spread + eps) * gain).astype(jnp.bfloat16)


def weight_kernel(token_hbm, embed_hbm, tail_hbm, qkv_hbm, out_hbm, embed, qkv, sems, out_sems):
    tiles, lanes, _ = embed.shape
    depth = lanes - tail_hbm.shape[0]
    copies, results = [], []
    for t in range(tiles):
        columns = pl.ds(t * TILE, TILE)
        copies.append(
            (
                pltpu.make_async_copy(
                    embed_hbm.at[pl.ds(0, depth), columns], embed.at[t, pl.ds(0, depth)], sems.at[2 * t]
                ),
                pltpu.make_async_copy(
                    tail_hbm.at[:, columns],
                    embed.at[t, pl.ds(depth, tail_hbm.shape[0])],
                    sems.at[2 * t + 1],
                ),
            )
        )
        results.append(
            pltpu.make_async_copy(embed.at[t], out_hbm.at[pl.ds(t * lanes, lanes)], out_sems.at[t])
        )
    copies.append((pltpu.make_async_copy(qkv_hbm, qkv, sems.at[2 * tiles]),))
    results.append(pltpu.make_async_copy(qkv, qkv_part(out_hbm, tiles * lanes, qkv), out_sems.at[tiles]))
    for pair in copies:
        for copy in pair:
            copy.start()
    for pair, result in zip(copies, results):
        for copy in pair:
            copy.wait()
        result.start()
    for result in results:
        result.wait()


def qkv_part(weights, first, qkv):
    return weights.at[pl.ds(first, qkv.shape[0]), pl.ds(0, qkv.shape[1])]


def tile_copies(weights_hbm, first, embed, sems):
    tiles, lanes, _ = embed.shape
    return [
        pltpu.make_async_copy(weights_hbm.at[pl.ds((first + t) * lanes, lanes)], embed.at[t], sems.at[t])
        for t in range(tiles)
    ]


def attend_kernel(
    x_ref, gain_ref, norm_ref, early_ref, weights_hbm, half_hbm,
    out_ref, late_ref, same_half_hbm, tokens, qkv, sems, qkv_sem,
):
    early, late = early_ref.shape[0], late_ref.shape[0]
    copies = tile_copies(weights_hbm, early, late_ref, sems)
    for copy in copies:
        copy.start()
    lanes = late_ref.shape[1]
    qkv_copy = pltpu.make_async_copy(
        qkv_part(weights_hbm, (early + late) * lanes, qkv), qkv, qkv_sem.at[0]
    )
    width = (early + late) * TILE
    x = x_ref[...]
    rows = x.shape[0]
    spans = [slice(at, at + TILE) for at in range(0, width, TILE)]
    total = jnp.zeros((rows, 128), jnp.float32)
    squares = jnp.zeros((rows, 128), jnp.float32)
    for t, span in enumerate(spans):
        if t == early:
            copies[0].wait()
            copies[1].wait()
            qkv_copy.start()
        if t == early + 2:
            for copy in copies[2:]:
                copy.wait()
        tile = early_ref[t] if t < early else late_ref[t - early]
        part = dot(x, tile).astype(jnp.bfloat16)
        tokens[:, span] = part
        part = part.astype(jnp.float32)
        total = lane_sums(part, total)
        squares = lane_sums(part * part, squares)
    mean = jnp.sum(total, axis=1, keepdims=True) / width
    squares = jnp.sum(squares, axis=1, keepdims=True) / width
    scale = lax.rsqrt(jnp.maximum(squares - mean * mean, 0.0) + eps)
    qkv_copy.wait()
    mixed = jnp.zeros((rows, qkv.shape[1]), jnp.float32)
    for span in spans:
        centre = tokens[:, span].astype(jnp.float32) - mean
        normed = (centre * scale * gain_ref[:, span].astype(jnp.float32)).astype(jnp.bfloat16)
        mixed = mixed + dot(normed, qkv[span, :])
    head = norm_ref.shape[1]
    queries = head_norm(mixed[:, :head], norm_ref[0:1, :])
    keys = head_norm(mixed[:, head : 2 * head], norm_ref[1:2, :])
    values = mixed[:, 2 * head :].astype(jnp.bfloat16)
    lane = iota((rows, 128), 1)
    flags = x[:, TAIL:].astype(jnp.float32)
    flags = jnp.where((lane >= SRC_AT) & (lane < SRC_END), flags, 0.0)
    live = jnp.sum(flags, axis=1, keepdims=True) > 0.5
    flags = flags.astype(jnp.bfloat16)
    same = dot(flags, flags, ((1,), (1,))) > 0.5
    scores = dot(queries, keys, ((1,), (1,))) / math.sqrt(head)
    scores = jnp.where(same, scores, -1e30)
    expo = jnp.exp(scores - jnp.max(scores, axis=1, keepdims=True))
    weights = (expo / jnp.sum(expo, axis=1, keepdims=True)).astype(jnp.bfloat16)
    out_ref[...] = jnp.where(live, dot(weights, values), 0.0).astype(jnp.bfloat16)


def embed_kernel(x_ref, early_ref, late_ref, out_ref):
    early, late = early_ref.shape[0], late_ref.shape[0]
    for t in range(early + late):
        tile = early_ref[t] if t < early else late_ref[t - early]
        out_ref[:, t * TILE : (t + 1) * TILE] = dot(x_ref[...], tile).astype(jnp.bfloat16)


def section_kernel(
    tokens_ref, attended_ref, mine_ref, other_ref, out_hbm, weight, out, sems
):
    half = mine_ref.shape[0]
    core = lax.axis_index("dp") % 2
    weight[pl.ds(pl.multiple_of(core * half, half), half), :] = mine_ref[...]
    weight[pl.ds(pl.multiple_of((1 - core) * half, half), half), :] = other_ref[...]
    results = []
    for t in range(out.shape[1] // TILE):
        span = slice(t * TILE, (t + 1) * TILE)
        part = tokens_ref[:, span].astype(jnp.float32)
        out[:, span] = (part + dot(attended_ref[...], weight[:, span])).astype(jnp.bfloat16)
        columns = pl.ds(t * TILE, TILE)
        result = pltpu.make_async_copy(out.at[:, columns], out_hbm.at[0, :, columns], sems.at[t])
        result.start()
        results.append(result)
    for result in results:
        result.wait()


VMEM = pl.BlockSpec(memory_space=pltpu.VMEM)
HBM = pl.BlockSpec(memory_space=pltpu.HBM)


def bf16(*shape):
    return jax.ShapeDtypeStruct(shape, jnp.bfloat16)


def call(kernel, out, in_specs, out_specs, scratch, limit, flops, aliases={}):
    return pl.pallas_call(
        kernel,
        out_shape=out,
        in_specs=in_specs,
        out_specs=out_specs,
        scratch_shapes=scratch,
        input_output_aliases=aliases,
        compiler_params=pltpu.CompilerParams(vmem_limit_bytes=limit * MIB),
        cost_estimate=pl.CostEstimate(flops=flops, bytes_accessed=MIB, transcendentals=0),
    )


def shards(
    patches,
    image_shape,
    keep_list,
    kept_count,
    dest_seq,
    embed_weight,
    pos_rows,
    pos_cols,
    ln_gain,
    qkv_weight,
    norm_gains,
    out_weight,
):
    groups = lax.axis_size("dp")
    segments = lax.axis_size("segment")
    images, patch_max, patch_width = patches.shape[1:]
    kept_max = keep_list.shape[2]
    seq_len = images * kept_max
    width = embed_weight.shape[1]
    head = out_weight.shape[1]
    tiles = width // TILE
    parts = 4
    onward = [(source, (source + 1) % segments) for source in range(segments)]
    pairs = [(source, source ^ 1) for source in range(groups)]
    dma = pltpu.SemaphoreType.DMA
    token = jax.ShapeDtypeStruct((8, 128), jnp.float32)

    packed, half, after_pack = call(
        pack_kernel,
        [bf16(groups, kept_max, LANES), bf16(head // 2, width), token],
        [HBM] * 6,
        [VMEM] * 3,
        [
            pltpu.SMEM((2, images), jnp.int32),
            pltpu.SMEM((1, images), jnp.int32),
            pltpu.SMEM((1, images), jnp.int32),
            pltpu.VMEM((images, kept_max), jnp.int32),
            pltpu.VMEM((images, patch_max, patch_width), jnp.bfloat16),
            dma((5,)),
            dma((parts,)),
        ],
        60,
        2 * images * kept_max * patch_max * LANES,
    )(image_shape[0].T, kept_count, dest_seq, keep_list[0], patches[0], out_weight[0])
    received = lax.all_to_all(packed, "dp", split_axis=0, concat_axis=0, tiled=True)

    half = lax.ppermute(half, "segment", onward)
    tail = jnp.concatenate(
        [
            embed_weight[LANES - 64 :],
            pos_rows,
            pos_cols,
            jnp.zeros((LANES - patch_width - 16, width), jnp.bfloat16),
        ],
        axis=0,
    )
    embed_scratch = pltpu.VMEM((tiles, LANES, TILE), jnp.bfloat16)
    qkv_scratch = pltpu.VMEM((width, 3 * head), jnp.bfloat16)
    weights = call(
        weight_kernel,
        bf16(STORE, TILE),
        [HBM] * 4,
        HBM,
        [embed_scratch, qkv_scratch, dma((2 * tiles + 1,)), dma((tiles + 1,))],
        20,
        MIB,
    )(after_pack, embed_weight, tail, qkv_weight[0])
    x, first_tiles = call(
        compact_kernel,
        [bf16(seq_len, LANES), bf16(EARLY, LANES, TILE)],
        [HBM, VMEM],
        [VMEM] * 2,
        [dma((EARLY,))],
        16,
        2 * seq_len * groups * kept_max * LANES,
    )(weights, received)
    next_x = lax.ppermute(x, "segment", onward)
    attended, other_tiles, half = call(
        attend_kernel,
        [bf16(seq_len, head), bf16(tiles - EARLY, LANES, TILE), bf16(head // 2, width)],
        [VMEM] * 4 + [HBM] * 2,
        [VMEM, VMEM, HBM],
        [
            pltpu.VMEM((seq_len, width), jnp.bfloat16),
            qkv_scratch,
            dma((tiles - EARLY,)),
            dma((1,)),
        ],
        34,
        2 * seq_len * width * (LANES + 3 * head),
        {5: 2},
    )(x, ln_gain, norm_gains[0], first_tiles, weights, half)
    next_attended = lax.ppermute(attended, "segment", onward)
    other = lax.ppermute(half, "dp", pairs)

    tokens = call(
        embed_kernel,
        bf16(seq_len, width),
        [VMEM] * 3,
        VMEM,
        [],
        16,
        2 * seq_len * width * LANES,
    )(next_x, first_tiles, other_tiles)
    return call(
        section_kernel,
        bf16(1, seq_len, width),
        [VMEM] * 4,
        HBM,
        [
            pltpu.VMEM((head, width), jnp.bfloat16),
            pltpu.VMEM((seq_len, width), jnp.bfloat16),
            dma((tiles,)),
        ],
        30,
        2 * seq_len * width * head,
    )(tokens, next_attended, half, other)


def solution(mesh):
    return jax.shard_map(
        shards,
        mesh=mesh,
        in_specs=(
            P("segment", "dp", None, None),
            P("segment", "dp", None),
            P("segment", "dp", None),
            P("segment", "dp"),
            P("segment", "dp"),
            P(),
            P(),
            P(),
            P("segment", None),
            P("segment", None, None),
            P("segment", None, None),
            P("segment", None, None),
        ),
        out_specs=P("segment", "dp", None),
        check_vma=False,
    )
```

```python
import math

import jax
import jax.numpy as jnp
from jax import lax
from jax.experimental import pallas as pl
from jax.experimental.pallas import tpu as pltpu
from jax.sharding import PartitionSpec as P

eps = 1e-06
LANES = 640
TAIL = 512
ROW_AT = 588 - TAIL
COL_AT = 596 - TAIL
SRC_AT = 604 - TAIL
SRC_END = 636 - TAIL
SIDE_MIN = 6
SIDE_MAX = 8
TILE = 1024
STORE = 20480
MIB = 1 << 20


def iota(shape, axis):
    return lax.broadcasted_iota(jnp.int32, shape, axis)


def dot(a, b, dims=((1,), (0,))):
    return lax.dot_general(a, b, (dims, ((), ())), preferred_element_type=jnp.float32)


def as_bf16(mask):
    return mask.astype(jnp.float32).astype(jnp.bfloat16)


def pack_kernel(
    shape_hbm, count_hbm, dest_hbm, keep_hbm, patches_hbm, weight_hbm, out_ref, half_ref, token_ref,
    shape, count, dest, keep, patches, sems, patch_sems,
):
    images, patch_max, _ = patches.shape
    kept_max = keep.shape[1]
    parts = patch_sems.shape[0]
    step = images // parts
    small = [
        pltpu.make_async_copy(source, target, sems.at[n])
        for n, (source, target) in enumerate(
            ((shape_hbm, shape), (count_hbm, count), (dest_hbm, dest), (keep_hbm, keep))
        )
    ]
    large = [
        pltpu.make_async_copy(
            patches_hbm.at[pl.ds(n * step, step)], patches.at[pl.ds(n * step, step)], patch_sems.at[n]
        )
        for n in range(parts)
    ]
    for copy in small + large:
        copy.start()
    device = lax.axis_index("dp")
    share = half_ref.shape[0]
    half = pltpu.make_async_copy(
        weight_hbm.at[pl.ds(pl.multiple_of(device % 2 * share, share), share)], half_ref, sems.at[4]
    )
    half.start()
    out_ref[...] = jnp.zeros_like(out_ref)
    token_ref[...] = jnp.zeros_like(token_ref)
    number = iota((patch_max, 128), 0)
    lane = iota((patch_max, 128), 1)
    source = lane == SRC_AT + device
    flags = {}
    for width in range(SIDE_MIN, SIDE_MAX + 1):
        row = jnp.zeros_like(number)
        for k in range(1, SIDE_MAX):
            row = row + (number >= k * width).astype(jnp.int32)
        col = number - row * width
        flags[width] = ((lane == ROW_AT + row) | (lane == COL_AT + col) | source).astype(jnp.float32)
    for copy in small:
        copy.wait()
    for g in range(images):
        if g % step == 0:
            large[g // step].wait()
        width = shape[1, g]
        own = flags[SIDE_MAX]
        for side in range(SIDE_MIN, SIDE_MAX):
            own = jnp.where(width == side, flags[side], own)
        picked = (iota((patch_max, kept_max), 0) == keep[g : g + 1, :]) & (
            iota((patch_max, kept_max), 1) < count[0, g]
        )
        picked = as_bf16(picked)
        there = dest[0, g]
        body = dot(picked, patches[g, :, :TAIL], ((0,), (0,)))
        out_ref[there, :, :TAIL] = body.astype(jnp.bfloat16)
        last = jnp.concatenate([patches[g, :, TAIL:], own.astype(jnp.bfloat16)[:, ROW_AT:]], axis=1)
        out_ref[there, :, TAIL:] = dot(picked, last, ((0,), (0,))).astype(jnp.bfloat16)
    half.wait()


def compact_kernel(weights_hbm, recv_ref, out_ref):
    sources, kept_max, lanes = recv_ref.shape
    total = sources * kept_max
    blocks = total // 128
    seq_len = out_ref.shape[0]
    received = recv_ref[...].reshape(total, lanes)
    at = iota((8, 128), 1)
    select = as_bf16((at >= SRC_AT) & (at < SRC_END))
    live = dot(select, received[:, TAIL:], ((1,), (1,)))
    group = iota((8, 128), 0)
    packed = jnp.zeros((8, 128), jnp.float32)
    for b in range(blocks):
        packed = jnp.where(group == b, live[:, b * 128 : (b + 1) * 128], packed)
    before = as_bf16(iota((128, 128), 0) < iota((128, 128), 1))
    within = dot(packed.astype(jnp.bfloat16), before)
    sums = jnp.sum(packed, axis=1, keepdims=True)
    base = jnp.zeros((8, 1), jnp.float32)
    for b in range(blocks - 1):
        base = base + jnp.where(iota((8, 1), 0) > b, sums[b : b + 1, :], 0.0)
    place = jnp.where(packed > 0.5, within + base, -1.0).astype(jnp.int32)
    slot = iota((seq_len, 128), 0)
    hot = jnp.concatenate([as_bf16(slot == place[b : b + 1, :]) for b in range(blocks)], axis=1)
    out_ref[...] = dot(hot, received).astype(jnp.bfloat16)


def lane_sums(values, sums):
    for at in range(0, values.shape[1], 128):
        sums = sums + values[:, at : at + 128]
    return sums


def head_norm(values, gain):
    centre = values - jnp.mean(values, axis=-1, keepdims=True)
    spread = jnp.mean(centre * centre, axis=-1, keepdims=True)
    return (centre * lax.rsqrt(spread + eps) * gain).astype(jnp.bfloat16)


def weight_kernel(token_hbm, embed_hbm, tail_hbm, qkv_hbm, out_hbm, embed, qkv, sems, out_sems):
    tiles, lanes, _ = embed.shape
    depth = lanes - tail_hbm.shape[0]
    copies, results = [], []
    for t in range(tiles):
        columns = pl.ds(t * TILE, TILE)
        copies.append(
            (
                pltpu.make_async_copy(
                    embed_hbm.at[pl.ds(0, depth), columns], embed.at[t, pl.ds(0, depth)], sems.at[2 * t]
                ),
                pltpu.make_async_copy(
                    tail_hbm.at[:, columns],
                    embed.at[t, pl.ds(depth, tail_hbm.shape[0])],
                    sems.at[2 * t + 1],
                ),
            )
        )
        results.append(
            pltpu.make_async_copy(embed.at[t], out_hbm.at[pl.ds(t * lanes, lanes)], out_sems.at[t])
        )
    copies.append((pltpu.make_async_copy(qkv_hbm, qkv, sems.at[2 * tiles]),))
    results.append(pltpu.make_async_copy(qkv, qkv_part(out_hbm, tiles * lanes, qkv), out_sems.at[tiles]))
    for pair in copies:
        for copy in pair:
            copy.start()
    for pair, result in zip(copies, results):
        for copy in pair:
            copy.wait()
        result.start()
    for result in results:
        result.wait()


def qkv_part(weights, first, qkv):
    return weights.at[pl.ds(first, qkv.shape[0]), pl.ds(0, qkv.shape[1])]


def tile_copies(weights_hbm, embed, sems):
    tiles, lanes, _ = embed.shape
    return [
        pltpu.make_async_copy(weights_hbm.at[pl.ds(t * lanes, lanes)], embed.at[t], sems.at[t])
        for t in range(tiles)
    ]


def attend_kernel(
    x_ref, gain_ref, norm_ref, weights_hbm, half_hbm,
    out_ref, embed, same_half_hbm, tokens, qkv, sems, qkv_sem,
):
    tiles, lanes, _ = embed.shape
    copies = tile_copies(weights_hbm, embed, sems)
    qkv_copy = pltpu.make_async_copy(qkv_part(weights_hbm, tiles * lanes, qkv), qkv, qkv_sem.at[0])
    width = tiles * TILE
    copies[0].start()
    copies[1].start()
    x = x_ref[...]
    rows = x.shape[0]
    spans = [slice(at, at + TILE) for at in range(0, width, TILE)]
    total = jnp.zeros((rows, 128), jnp.float32)
    squares = jnp.zeros((rows, 128), jnp.float32)
    for t, span in enumerate(spans):
        if t < 2:
            copies[t].wait()
            for later in copies[2 * t + 2 : 2 * t + 4]:
                later.start()
        elif t % 2 == 0:
            copies[t].wait()
            copies[t + 1].wait()
            if t == 2:
                qkv_copy.start()
        part = dot(x, embed[t]).astype(jnp.bfloat16)
        tokens[:, span] = part
        part = part.astype(jnp.float32)
        total = lane_sums(part, total)
        squares = lane_sums(part * part, squares)
    mean = jnp.sum(total, axis=1, keepdims=True) / width
    squares = jnp.sum(squares, axis=1, keepdims=True) / width
    scale = lax.rsqrt(jnp.maximum(squares - mean * mean, 0.0) + eps)
    qkv_copy.wait()
    mixed = jnp.zeros((rows, qkv.shape[1]), jnp.float32)
    for span in spans:
        centre = tokens[:, span].astype(jnp.float32) - mean
        normed = (centre * scale * gain_ref[:, span].astype(jnp.float32)).astype(jnp.bfloat16)
        mixed = mixed + dot(normed, qkv[span, :])
    head = norm_ref.shape[1]
    queries = head_norm(mixed[:, :head], norm_ref[0:1, :])
    keys = head_norm(mixed[:, head : 2 * head], norm_ref[1:2, :])
    values = mixed[:, 2 * head :].astype(jnp.bfloat16)
    lane = iota((rows, 128), 1)
    flags = x[:, TAIL:].astype(jnp.float32)
    flags = jnp.where((lane >= SRC_AT) & (lane < SRC_END), flags, 0.0)
    live = jnp.sum(flags, axis=1, keepdims=True) > 0.5
    flags = flags.astype(jnp.bfloat16)
    for at in range(0, rows, 128):
        here = slice(at, at + 128)
        first = min(max(at - 64, 0), rows - 256)
        near = slice(first, first + 256)
        same = dot(flags[here], flags[near], ((1,), (1,))) > 0.5
        scores = dot(queries[here], keys[near], ((1,), (1,))) * (1.0 / math.sqrt(head))
        scores = jnp.where(same, scores, -1e30)
        expo = jnp.exp(scores - jnp.max(scores, axis=1, keepdims=True))
        weights = (expo * (1.0 / jnp.sum(expo, axis=1, keepdims=True))).astype(jnp.bfloat16)
        attended = jnp.where(live[here], dot(weights, values[near]), 0.0)
        out_ref[here, :] = attended.astype(jnp.bfloat16)


def embed_kernel(x_ref, embed_ref, out_ref):
    for t in range(embed_ref.shape[0]):
        span = slice(t * TILE, (t + 1) * TILE)
        out_ref[:, span] = dot(x_ref[...], embed_ref[t]).astype(jnp.bfloat16)


def section_kernel(
    tokens_ref, attended_ref, mine_ref, other_ref, out_hbm, weight, out, sems
):
    half = mine_ref.shape[0]
    core = lax.axis_index("dp") % 2
    weight[pl.ds(pl.multiple_of(core * half, half), half), :] = mine_ref[...]
    weight[pl.ds(pl.multiple_of((1 - core) * half, half), half), :] = other_ref[...]
    results = []
    for t in range(out.shape[1] // TILE):
        span = slice(t * TILE, (t + 1) * TILE)
        part = tokens_ref[:, span].astype(jnp.float32)
        out[:, span] = (part + dot(attended_ref[...], weight[:, span])).astype(jnp.bfloat16)
        columns = pl.ds(t * TILE, TILE)
        result = pltpu.make_async_copy(out.at[:, columns], out_hbm.at[0, :, columns], sems.at[t])
        result.start()
        results.append(result)
    for result in results:
        result.wait()


VMEM = pl.BlockSpec(memory_space=pltpu.VMEM)
HBM = pl.BlockSpec(memory_space=pltpu.HBM)


def bf16(*shape):
    return jax.ShapeDtypeStruct(shape, jnp.bfloat16)


def call(kernel, out, in_specs, out_specs, scratch, limit, flops, aliases={}):
    return pl.pallas_call(
        kernel,
        out_shape=out,
        in_specs=in_specs,
        out_specs=out_specs,
        scratch_shapes=scratch,
        input_output_aliases=aliases,
        compiler_params=pltpu.CompilerParams(vmem_limit_bytes=limit * MIB),
        cost_estimate=pl.CostEstimate(flops=flops, bytes_accessed=MIB, transcendentals=0),
    )


def shards(
    patches,
    image_shape,
    keep_list,
    kept_count,
    dest_seq,
    embed_weight,
    pos_rows,
    pos_cols,
    ln_gain,
    qkv_weight,
    norm_gains,
    out_weight,
):
    groups = lax.axis_size("dp")
    segments = lax.axis_size("segment")
    images, patch_max, patch_width = patches.shape[1:]
    kept_max = keep_list.shape[2]
    seq_len = images * kept_max
    width = embed_weight.shape[1]
    head = out_weight.shape[1]
    tiles = width // TILE
    parts = 4
    onward = [(source, (source + 1) % segments) for source in range(segments)]
    pairs = [(source, source ^ 1) for source in range(groups)]
    dma = pltpu.SemaphoreType.DMA
    token = jax.ShapeDtypeStruct((8, 128), jnp.float32)

    packed, half, after_pack = call(
        pack_kernel,
        [bf16(groups, kept_max, LANES), bf16(head // 2, width), token],
        [HBM] * 6,
        [VMEM] * 3,
        [
            pltpu.SMEM((2, images), jnp.int32),
            pltpu.SMEM((1, images), jnp.int32),
            pltpu.SMEM((1, images), jnp.int32),
            pltpu.VMEM((images, kept_max), jnp.int32),
            pltpu.VMEM((images, patch_max, patch_width), jnp.bfloat16),
            dma((5,)),
            dma((parts,)),
        ],
        60,
        2 * images * kept_max * patch_max * LANES,
    )(image_shape[0].T, kept_count, dest_seq, keep_list[0], patches[0], out_weight[0])
    received = lax.all_to_all(packed, "dp", split_axis=0, concat_axis=0, tiled=True)

    half = lax.ppermute(half, "segment", onward)
    tail = jnp.concatenate(
        [
            embed_weight[LANES - 64 :],
            pos_rows,
            pos_cols,
            jnp.zeros((LANES - patch_width - 16, width), jnp.bfloat16),
        ],
        axis=0,
    )
    embed_scratch = pltpu.VMEM((tiles, LANES, TILE), jnp.bfloat16)
    qkv_scratch = pltpu.VMEM((width, 3 * head), jnp.bfloat16)
    weights = call(
        weight_kernel,
        bf16(STORE, TILE),
        [HBM] * 4,
        HBM,
        [embed_scratch, qkv_scratch, dma((2 * tiles + 1,)), dma((tiles + 1,))],
        20,
        MIB,
    )(after_pack, embed_weight, tail, qkv_weight[0])
    x = call(
        compact_kernel,
        bf16(seq_len, LANES),
        [HBM, VMEM],
        VMEM,
        [],
        16,
        2 * seq_len * groups * kept_max * LANES,
    )(weights, received)
    next_x = lax.ppermute(x, "segment", onward)
    attended, embed, half = call(
        attend_kernel,
        [bf16(seq_len, head), bf16(tiles, LANES, TILE), bf16(head // 2, width)],
        [VMEM] * 3 + [HBM] * 2,
        [VMEM, VMEM, HBM],
        [
            pltpu.VMEM((seq_len, width), jnp.bfloat16),
            qkv_scratch,
            dma((tiles,)),
            dma((1,)),
        ],
        34,
        2 * seq_len * width * (LANES + 3 * head),
        {4: 2},
    )(x, ln_gain, norm_gains[0], weights, half)
    next_attended = lax.ppermute(attended, "segment", onward)
    other = lax.ppermute(half, "dp", pairs)

    tokens = call(
        embed_kernel,
        bf16(seq_len, width),
        [VMEM] * 2,
        VMEM,
        [],
        16,
        2 * seq_len * width * LANES,
    )(next_x, embed)
    return call(
        section_kernel,
        bf16(1, seq_len, width),
        [VMEM] * 4,
        HBM,
        [
            pltpu.VMEM((head, width), jnp.bfloat16),
            pltpu.VMEM((seq_len, width), jnp.bfloat16),
            dma((tiles,)),
        ],
        30,
        2 * seq_len * width * head,
    )(tokens, next_attended, half, other)


def solution(mesh):
    return jax.shard_map(
        shards,
        mesh=mesh,
        in_specs=(
            P("segment", "dp", None, None),
            P("segment", "dp", None),
            P("segment", "dp", None),
            P("segment", "dp"),
            P("segment", "dp"),
            P(),
            P(),
            P(),
            P("segment", None),
            P("segment", None, None),
            P("segment", None, None),
            P("segment", None, None),
        ),
        out_specs=P("segment", "dp", None),
        check_vma=False,
    )
```

```python
import math

import jax
import jax.numpy as jnp
from jax import lax
from jax.experimental import pallas as pl
from jax.experimental.pallas import tpu as pltpu
from jax.sharding import PartitionSpec as P

eps = 1e-06
LANES = 640
TAIL = 512
ROW_AT = 588 - TAIL
COL_AT = 596 - TAIL
SRC_AT = 604 - TAIL
SRC_END = 636 - TAIL
SIDE_MIN = 6
SIDE_MAX = 8
TILE = 1024
STORE = 20480
MIB = 1 << 20


def iota(shape, axis):
    return lax.broadcasted_iota(jnp.int32, shape, axis)


def dot(a, b, dims=((1,), (0,))):
    return lax.dot_general(a, b, (dims, ((), ())), preferred_element_type=jnp.float32)


def as_bf16(mask):
    return mask.astype(jnp.float32).astype(jnp.bfloat16)


def pack_kernel(
    shape_hbm, count_hbm, dest_hbm, keep_hbm, patches_hbm, weight_hbm, out_ref, half_ref, token_ref,
    shape, count, dest, keep, patches, sems, patch_sems,
):
    images, patch_max, _ = patches.shape
    kept_max = keep.shape[1]
    parts = patch_sems.shape[0]
    step = images // parts
    small = [
        pltpu.make_async_copy(source, target, sems.at[n])
        for n, (source, target) in enumerate(
            ((shape_hbm, shape), (count_hbm, count), (dest_hbm, dest), (keep_hbm, keep))
        )
    ]
    large = [
        pltpu.make_async_copy(
            patches_hbm.at[pl.ds(n * step, step)], patches.at[pl.ds(n * step, step)], patch_sems.at[n]
        )
        for n in range(parts)
    ]
    for copy in small + large:
        copy.start()
    device = lax.axis_index("dp")
    share = half_ref.shape[0]
    half = pltpu.make_async_copy(
        weight_hbm.at[pl.ds(pl.multiple_of(device % 2 * share, share), share)], half_ref, sems.at[4]
    )
    half.start()
    out_ref[...] = jnp.zeros_like(out_ref)
    token_ref[...] = jnp.zeros_like(token_ref)
    number = iota((patch_max, 128), 0)
    lane = iota((patch_max, 128), 1)
    source = lane == SRC_AT + device
    flags = {}
    for width in range(SIDE_MIN, SIDE_MAX + 1):
        row = jnp.zeros_like(number)
        for k in range(1, SIDE_MAX):
            row = row + (number >= k * width).astype(jnp.int32)
        col = number - row * width
        flags[width] = ((lane == ROW_AT + row) | (lane == COL_AT + col) | source).astype(jnp.float32)
    for copy in small:
        copy.wait()
    for g in range(images):
        if g % step == 0:
            large[g // step].wait()
        width = shape[1, g]
        own = flags[SIDE_MAX]
        for side in range(SIDE_MIN, SIDE_MAX):
            own = jnp.where(width == side, flags[side], own)
        picked = (iota((patch_max, kept_max), 0) == keep[g : g + 1, :]) & (
            iota((patch_max, kept_max), 1) < count[0, g]
        )
        picked = as_bf16(picked)
        there = dest[0, g]
        body = dot(picked, patches[g, :, :TAIL], ((0,), (0,)))
        out_ref[there, :, :TAIL] = body.astype(jnp.bfloat16)
        last = jnp.concatenate([patches[g, :, TAIL:], own.astype(jnp.bfloat16)[:, ROW_AT:]], axis=1)
        out_ref[there, :, TAIL:] = dot(picked, last, ((0,), (0,))).astype(jnp.bfloat16)
    half.wait()


def compact_kernel(weights_hbm, recv_ref, out_ref):
    sources, kept_max, lanes = recv_ref.shape
    total = sources * kept_max
    blocks = total // 128
    seq_len = out_ref.shape[0]
    received = recv_ref[...].reshape(total, lanes)
    at = iota((8, 128), 1)
    select = as_bf16((at >= SRC_AT) & (at < SRC_END))
    live = dot(select, received[:, TAIL:], ((1,), (1,)))
    group = iota((8, 128), 0)
    packed = jnp.zeros((8, 128), jnp.float32)
    for b in range(blocks):
        packed = jnp.where(group == b, live[:, b * 128 : (b + 1) * 128], packed)
    before = as_bf16(iota((128, 128), 0) < iota((128, 128), 1))
    within = dot(packed.astype(jnp.bfloat16), before)
    sums = jnp.sum(packed, axis=1, keepdims=True)
    base = jnp.zeros((8, 1), jnp.float32)
    for b in range(blocks - 1):
        base = base + jnp.where(iota((8, 1), 0) > b, sums[b : b + 1, :], 0.0)
    place = jnp.where(packed > 0.5, within + base, -1.0).astype(jnp.int32)
    slot = iota((seq_len, 128), 0)
    hot = jnp.concatenate([as_bf16(slot == place[b : b + 1, :]) for b in range(blocks)], axis=1)
    out_ref[...] = dot(hot, received).astype(jnp.bfloat16)


def lane_sums(values, sums):
    for at in range(0, values.shape[1], 128):
        sums = sums + values[:, at : at + 128]
    return sums


def head_norm(values, gain):
    centre = values - jnp.mean(values, axis=-1, keepdims=True)
    spread = jnp.mean(centre * centre, axis=-1, keepdims=True)
    return (centre * lax.rsqrt(spread + eps) * gain).astype(jnp.bfloat16)


def weight_kernel(token_hbm, embed_hbm, tail_hbm, qkv_hbm, out_hbm, embed, qkv, sems, out_sems):
    tiles, lanes, _ = embed.shape
    depth = lanes - tail_hbm.shape[0]
    copies, results = [], []
    for t in range(tiles):
        columns = pl.ds(t * TILE, TILE)
        copies.append(
            (
                pltpu.make_async_copy(
                    embed_hbm.at[pl.ds(0, depth), columns], embed.at[t, pl.ds(0, depth)], sems.at[2 * t]
                ),
                pltpu.make_async_copy(
                    tail_hbm.at[:, columns],
                    embed.at[t, pl.ds(depth, tail_hbm.shape[0])],
                    sems.at[2 * t + 1],
                ),
            )
        )
        results.append(
            pltpu.make_async_copy(embed.at[t], out_hbm.at[pl.ds(t * lanes, lanes)], out_sems.at[t])
        )
    copies.append((pltpu.make_async_copy(qkv_hbm, qkv, sems.at[2 * tiles]),))
    results.append(pltpu.make_async_copy(qkv, qkv_part(out_hbm, tiles * lanes, qkv), out_sems.at[tiles]))
    for pair in copies:
        for copy in pair:
            copy.start()
    for pair, result in zip(copies, results):
        for copy in pair:
            copy.wait()
        result.start()
    for result in results:
        result.wait()


def qkv_part(weights, first, qkv):
    return weights.at[pl.ds(first, qkv.shape[0]), pl.ds(0, qkv.shape[1])]


def tile_copies(weights_hbm, embed, sems):
    tiles, lanes, _ = embed.shape
    return [
        pltpu.make_async_copy(weights_hbm.at[pl.ds(t * lanes, lanes)], embed.at[t], sems.at[t])
        for t in range(tiles)
    ]


def attend_kernel(
    x_ref, gain_ref, norm_ref, weights_hbm, half_hbm,
    out_ref, embed, same_half_hbm, tokens, qkv, sems, qkv_sem,
):
    tiles, lanes, _ = embed.shape
    copies = tile_copies(weights_hbm, embed, sems)
    qkv_copy = pltpu.make_async_copy(qkv_part(weights_hbm, tiles * lanes, qkv), qkv, qkv_sem.at[0])
    width = tiles * TILE
    copies[0].start()
    copies[1].start()
    x = x_ref[...]
    rows = x.shape[0]
    spans = [slice(at, at + TILE) for at in range(0, width, TILE)]
    total = jnp.zeros((rows, 128), jnp.float32)
    squares = jnp.zeros((rows, 128), jnp.float32)
    for t, span in enumerate(spans):
        if t < 2:
            copies[t].wait()
            for later in copies[2 * t + 2 : 2 * t + 4]:
                later.start()
        elif t % 2 == 0:
            copies[t].wait()
            copies[t + 1].wait()
            if t == 2:
                qkv_copy.start()
        part = dot(x, embed[t]).astype(jnp.bfloat16)
        tokens[:, span] = part
        part = part.astype(jnp.float32)
        total = lane_sums(part, total)
        squares = lane_sums(part * part, squares)
    mean = jnp.sum(total, axis=1, keepdims=True) / width
    squares = jnp.sum(squares, axis=1, keepdims=True) / width
    scale = lax.rsqrt(jnp.maximum(squares - mean * mean, 0.0) + eps)
    qkv_copy.wait()
    mixed = jnp.zeros((rows, qkv.shape[1]), jnp.float32)
    for span in spans:
        centre = tokens[:, span].astype(jnp.float32) - mean
        normed = (centre * scale * gain_ref[:, span].astype(jnp.float32)).astype(jnp.bfloat16)
        mixed = mixed + dot(normed, qkv[span, :])
    head = norm_ref.shape[1]
    queries = head_norm(mixed[:, :head], norm_ref[0:1, :])
    keys = head_norm(mixed[:, head : 2 * head], norm_ref[1:2, :])
    values = mixed[:, 2 * head :].astype(jnp.bfloat16)
    lane = iota((rows, 128), 1)
    flags = x[:, TAIL:].astype(jnp.float32)
    flags = jnp.where((lane >= SRC_AT) & (lane < SRC_END), flags, 0.0)
    live = jnp.sum(flags, axis=1, keepdims=True) > 0.5
    flags = flags.astype(jnp.bfloat16)
    for at in range(0, rows, 128):
        here = slice(at, at + 128)
        first = min(max(at - 64, 0), rows - 256)
        near = slice(first, first + 256)
        same = dot(flags[here], flags[near], ((1,), (1,))) > 0.5
        scores = dot(queries[here], keys[near], ((1,), (1,))) * (1.0 / math.sqrt(head))
        scores = jnp.where(same, scores, -1e30)
        expo = jnp.exp(scores - jnp.max(scores, axis=1, keepdims=True))
        weights = (expo * (1.0 / jnp.sum(expo, axis=1, keepdims=True))).astype(jnp.bfloat16)
        attended = jnp.where(live[here], dot(weights, values[near]), 0.0)
        out_ref[here, :] = attended.astype(jnp.bfloat16)


def embed_kernel(x_ref, embed_ref, out_ref):
    for t in range(embed_ref.shape[0]):
        span = slice(t * TILE, (t + 1) * TILE)
        out_ref[:, span] = dot(x_ref[:, :TAIL], embed_ref[t, :TAIL])


def section_kernel(
    part_ref, x_ref, attended_ref, embed_ref, mine_ref, other_ref, out_hbm, weight, out, sems
):
    half = mine_ref.shape[0]
    last = x_ref.shape[1] - TAIL
    core = lax.axis_index("dp") % 2
    weight[pl.ds(pl.multiple_of(last + core * half, half), half), :] = mine_ref[...]
    weight[pl.ds(pl.multiple_of(last + (1 - core) * half, half), half), :] = other_ref[...]
    both = jnp.concatenate([x_ref[:, TAIL:], attended_ref[...]], axis=1)
    results = []
    for t in range(out.shape[1] // TILE):
        span = slice(t * TILE, (t + 1) * TILE)
        weight[:last, span] = embed_ref[t, TAIL:]
        out[:, span] = (part_ref[:, span] + dot(both, weight[:, span])).astype(jnp.bfloat16)
        columns = pl.ds(t * TILE, TILE)
        result = pltpu.make_async_copy(out.at[:, columns], out_hbm.at[0, :, columns], sems.at[t])
        result.start()
        results.append(result)
    for result in results:
        result.wait()


VMEM = pl.BlockSpec(memory_space=pltpu.VMEM)
HBM = pl.BlockSpec(memory_space=pltpu.HBM)


def bf16(*shape):
    return jax.ShapeDtypeStruct(shape, jnp.bfloat16)


def call(kernel, out, in_specs, out_specs, scratch, limit, flops, aliases={}):
    return pl.pallas_call(
        kernel,
        out_shape=out,
        in_specs=in_specs,
        out_specs=out_specs,
        scratch_shapes=scratch,
        input_output_aliases=aliases,
        compiler_params=pltpu.CompilerParams(vmem_limit_bytes=limit * MIB),
        cost_estimate=pl.CostEstimate(flops=flops, bytes_accessed=MIB, transcendentals=0),
    )


def shards(
    patches,
    image_shape,
    keep_list,
    kept_count,
    dest_seq,
    embed_weight,
    pos_rows,
    pos_cols,
    ln_gain,
    qkv_weight,
    norm_gains,
    out_weight,
):
    groups = lax.axis_size("dp")
    segments = lax.axis_size("segment")
    images, patch_max, patch_width = patches.shape[1:]
    kept_max = keep_list.shape[2]
    seq_len = images * kept_max
    width = embed_weight.shape[1]
    head = out_weight.shape[1]
    tiles = width // TILE
    parts = 4
    onward = [(source, (source + 1) % segments) for source in range(segments)]
    pairs = [(source, source ^ 1) for source in range(groups)]
    dma = pltpu.SemaphoreType.DMA
    token = jax.ShapeDtypeStruct((8, 128), jnp.float32)

    packed, half, after_pack = call(
        pack_kernel,
        [bf16(groups, kept_max, LANES), bf16(head // 2, width), token],
        [HBM] * 6,
        [VMEM] * 3,
        [
            pltpu.SMEM((2, images), jnp.int32),
            pltpu.SMEM((1, images), jnp.int32),
            pltpu.SMEM((1, images), jnp.int32),
            pltpu.VMEM((images, kept_max), jnp.int32),
            pltpu.VMEM((images, patch_max, patch_width), jnp.bfloat16),
            dma((5,)),
            dma((parts,)),
        ],
        60,
        2 * images * kept_max * patch_max * LANES,
    )(image_shape[0].T, kept_count, dest_seq, keep_list[0], patches[0], out_weight[0])
    received = lax.all_to_all(packed, "dp", split_axis=0, concat_axis=0, tiled=True)

    half = lax.ppermute(half, "segment", onward)
    tail = jnp.concatenate(
        [
            embed_weight[LANES - 64 :],
            pos_rows,
            pos_cols,
            jnp.zeros((LANES - patch_width - 16, width), jnp.bfloat16),
        ],
        axis=0,
    )
    embed_scratch = pltpu.VMEM((tiles, LANES, TILE), jnp.bfloat16)
    qkv_scratch = pltpu.VMEM((width, 3 * head), jnp.bfloat16)
    weights = call(
        weight_kernel,
        bf16(STORE, TILE),
        [HBM] * 4,
        HBM,
        [embed_scratch, qkv_scratch, dma((2 * tiles + 1,)), dma((tiles + 1,))],
        20,
        MIB,
    )(after_pack, embed_weight, tail, qkv_weight[0])
    x = call(
        compact_kernel,
        bf16(seq_len, LANES),
        [HBM, VMEM],
        VMEM,
        [],
        16,
        2 * seq_len * groups * kept_max * LANES,
    )(weights, received)
    next_x = lax.ppermute(x, "segment", onward)
    attended, embed, half = call(
        attend_kernel,
        [bf16(seq_len, head), bf16(tiles, LANES, TILE), bf16(head // 2, width)],
        [VMEM] * 3 + [HBM] * 2,
        [VMEM, VMEM, HBM],
        [
            pltpu.VMEM((seq_len, width), jnp.bfloat16),
            qkv_scratch,
            dma((tiles,)),
            dma((1,)),
        ],
        34,
        2 * seq_len * width * (LANES + 3 * head),
        {4: 2},
    )(x, ln_gain, norm_gains[0], weights, half)
    next_attended = lax.ppermute(attended, "segment", onward)
    other = lax.ppermute(half, "dp", pairs)

    part = call(
        embed_kernel,
        jax.ShapeDtypeStruct((seq_len, width), jnp.float32),
        [VMEM] * 2,
        VMEM,
        [],
        24,
        2 * seq_len * width * LANES,
    )(next_x, embed)
    return call(
        section_kernel,
        bf16(1, seq_len, width),
        [VMEM] * 6,
        HBM,
        [
            pltpu.VMEM((LANES - TAIL + head, width), jnp.bfloat16),
            pltpu.VMEM((seq_len, width), jnp.bfloat16),
            dma((tiles,)),
        ],
        30,
        2 * seq_len * width * head,
    )(part, next_x, next_attended, embed, half, other)


def solution(mesh):
    return jax.shard_map(
        shards,
        mesh=mesh,
        in_specs=(
            P("segment", "dp", None, None),
            P("segment", "dp", None),
            P("segment", "dp", None),
            P("segment", "dp"),
            P("segment", "dp"),
            P(),
            P(),
            P(),
            P("segment", None),
            P("segment", None, None),
            P("segment", None, None),
            P("segment", None, None),
        ),
        out_specs=P("segment", "dp", None),
        check_vma=False,
    )
```

```python
import math

import jax
import jax.numpy as jnp
from jax import lax
from jax.experimental import pallas as pl
from jax.experimental.pallas import tpu as pltpu
from jax.sharding import PartitionSpec as P

eps = 1e-06
LANES = 640
TAIL = 512
ROW_AT = 588 - TAIL
COL_AT = 596 - TAIL
SRC_AT = 604 - TAIL
SRC_END = 636 - TAIL
SIDE_MIN = 6
SIDE_MAX = 8
TILE = 1024
STORE = 20480
MIB = 1 << 20


def iota(shape, axis):
    return lax.broadcasted_iota(jnp.int32, shape, axis)


def dot(a, b, dims=((1,), (0,))):
    return lax.dot_general(a, b, (dims, ((), ())), preferred_element_type=jnp.float32)


def as_bf16(mask):
    return mask.astype(jnp.float32).astype(jnp.bfloat16)


def pack_kernel(
    shape_hbm, count_hbm, dest_hbm, keep_hbm, patches_hbm, weight_hbm, out_ref, half_hbm, token_ref,
    shape, count, dest, keep, patches, half, sems, patch_sems,
):
    images, patch_max, _ = patches.shape
    kept_max = keep.shape[1]
    parts = patch_sems.shape[0]
    step = images // parts
    small = [
        pltpu.make_async_copy(source, target, sems.at[n])
        for n, (source, target) in enumerate(
            ((shape_hbm, shape), (count_hbm, count), (dest_hbm, dest), (keep_hbm, keep))
        )
    ]
    large = [
        pltpu.make_async_copy(
            patches_hbm.at[pl.ds(n * step, step)], patches.at[pl.ds(n * step, step)], patch_sems.at[n]
        )
        for n in range(parts)
    ]
    for copy in small + large:
        copy.start()
    device = lax.axis_index("dp")
    share = half.shape[0]
    half_in = pltpu.make_async_copy(
        weight_hbm.at[pl.ds(pl.multiple_of(device % 2 * share, share), share)], half, sems.at[4]
    )
    half_out = pltpu.make_async_copy(half, half_hbm, sems.at[5])
    half_in.start()
    out_ref[...] = jnp.zeros_like(out_ref)
    token_ref[...] = jnp.zeros_like(token_ref)
    number = iota((patch_max, 128), 0)
    lane = iota((patch_max, 128), 1)
    source = lane == SRC_AT + device
    flags = {}
    for width in range(SIDE_MIN, SIDE_MAX + 1):
        row = jnp.zeros_like(number)
        for k in range(1, SIDE_MAX):
            row = row + (number >= k * width).astype(jnp.int32)
        col = number - row * width
        flags[width] = ((lane == ROW_AT + row) | (lane == COL_AT + col) | source).astype(jnp.float32)
    for copy in small:
        copy.wait()
    unit = as_bf16(iota((images, images), 0) == iota((images, images), 1))
    listed = dot(keep[...].astype(jnp.float32).astype(jnp.bfloat16), unit, ((0,), (0,))).astype(jnp.int32)
    for g in range(images):
        if g % step == 0:
            large[g // step].wait()
        width = shape[1, g]
        own = flags[SIDE_MAX]
        for side in range(SIDE_MIN, SIDE_MAX):
            own = jnp.where(width == side, flags[side], own)
        picked = (iota((kept_max, patch_max), 1) == listed[:, g : g + 1]) & (
            iota((kept_max, patch_max), 0) < count[0, g]
        )
        picked = as_bf16(picked)
        there = dest[0, g]
        out_ref[there, :, :TAIL] = dot(picked, patches[g, :, :TAIL]).astype(jnp.bfloat16)
        last = jnp.concatenate([patches[g, :, TAIL:], own.astype(jnp.bfloat16)[:, ROW_AT:]], axis=1)
        out_ref[there, :, TAIL:] = dot(picked, last).astype(jnp.bfloat16)
        if g == images // 2:
            half_in.wait()
            half_out.start()
    half_out.wait()


def compact_kernel(weights_hbm, recv_ref, out_ref, early_ref, sems):
    (early,) = tile_copies(weights_hbm, 1, early_ref, sems)
    early.start()
    sources, kept_max, lanes = recv_ref.shape
    total = sources * kept_max
    blocks = total // 128
    seq_len = out_ref.shape[0]
    received = recv_ref[...].reshape(total, lanes)
    at = iota((8, 128), 1)
    select = as_bf16((at >= SRC_AT) & (at < SRC_END))
    live = dot(select, received[:, TAIL:], ((1,), (1,)))
    group = iota((8, 128), 0)
    packed = jnp.zeros((8, 128), jnp.float32)
    for b in range(blocks):
        packed = jnp.where(group == b, live[:, b * 128 : (b + 1) * 128], packed)
    before = as_bf16(iota((128, 128), 0) < iota((128, 128), 1))
    within = dot(packed.astype(jnp.bfloat16), before)
    sums = jnp.sum(packed, axis=1, keepdims=True)
    base = jnp.zeros((8, 1), jnp.float32)
    for b in range(blocks - 1):
        base = base + jnp.where(iota((8, 1), 0) > b, sums[b : b + 1, :], 0.0)
    place = jnp.where(packed > 0.5, within + base, -1.0).astype(jnp.int32)
    slot = iota((seq_len, 128), 0)
    hot = jnp.concatenate([as_bf16(slot == place[b : b + 1, :]) for b in range(blocks)], axis=1)
    out_ref[...] = dot(hot, received).astype(jnp.bfloat16)
    early.wait()


def lane_sums(values, sums):
    for at in range(0, values.shape[1], 128):
        sums = sums + values[:, at : at + 128]
    return sums


def head_norm(values, gain):
    centre = values - jnp.mean(values, axis=-1, keepdims=True)
    spread = jnp.mean(centre * centre, axis=-1, keepdims=True)
    return (centre * lax.rsqrt(spread + eps) * gain).astype(jnp.bfloat16)


def weight_kernel(token_hbm, embed_ref, tail_ref, qkv_ref, out_hbm, tile_ref, sems):
    tail = tail_ref.shape[0]
    depth = LANES - tail
    tiles = embed_ref.shape[1] // TILE
    copies = []
    for t in range(tiles):
        columns = pl.ds(t * TILE, TILE)
        for source, first, rows in ((embed_ref, t * LANES, depth), (tail_ref, t * LANES + depth, tail)):
            copies.append(
                pltpu.make_async_copy(
                    source.at[pl.ds(0, rows), columns], out_hbm.at[pl.ds(first, rows)], sems.at[len(copies)]
                )
            )
    columns = pl.ds(0, TILE)
    for source, first, rows in ((embed_ref, 0, depth), (tail_ref, depth, tail)):
        copies.append(
            pltpu.make_async_copy(
                source.at[pl.ds(0, rows), columns],
                tile_ref.at[0, pl.ds(first, rows)],
                sems.at[len(copies)],
            )
        )
    copies.append(
        pltpu.make_async_copy(qkv_ref, qkv_part(out_hbm, tiles * LANES, qkv_ref), sems.at[len(copies)])
    )
    for copy in copies:
        copy.start()
    for copy in copies:
        copy.wait()


def qkv_part(weights, first, qkv):
    return weights.at[pl.ds(first, qkv.shape[0]), pl.ds(0, qkv.shape[1])]


def tile_copies(weights_hbm, first, embed, sems):
    tiles, lanes, _ = embed.shape
    return [
        pltpu.make_async_copy(weights_hbm.at[pl.ds((first + t) * lanes, lanes)], embed.at[t], sems.at[t])
        for t in range(tiles)
    ]


def hand_on_kernel(token_hbm, half_hbm, same_half_hbm):
    pass


def attend_kernel(
    x_ref, gain_ref, norm_ref, tile_ref, early_ref, weights_hbm, out_ref, late_ref, token_ref,
    tokens, qkv, sems, qkv_sem,
):
    late, lanes, _ = late_ref.shape
    copies = tile_copies(weights_hbm, 2, late_ref, sems)
    qkv_copy = pltpu.make_async_copy(qkv_part(weights_hbm, (2 + late) * lanes, qkv), qkv, qkv_sem.at[0])
    width = (2 + late) * TILE
    copies[0].start()
    copies[1].start()
    token_ref[...] = jnp.zeros_like(token_ref)
    x = x_ref[...]
    rows = x.shape[0]
    spans = [slice(at, at + TILE) for at in range(0, width, TILE)]
    total = jnp.zeros((rows, 128), jnp.float32)
    squares = jnp.zeros((rows, 128), jnp.float32)
    for t, span in enumerate(spans):
        if t == 1:
            copies[2].start()
            copies[3].start()
        if t == 2:
            copies[0].wait()
            copies[1].wait()
            qkv_copy.start()
        if t == 4:
            copies[2].wait()
            copies[3].wait()
        tile = (tile_ref[0], early_ref[0])[t] if t < 2 else late_ref[t - 2]
        part = dot(x, tile).astype(jnp.bfloat16)
        tokens[:, span] = part
        part = part.astype(jnp.float32)
        total = lane_sums(part, total)
        squares = lane_sums(part * part, squares)
    mean = jnp.sum(total, axis=1, keepdims=True) / width
    squares = jnp.sum(squares, axis=1, keepdims=True) / width
    scale = lax.rsqrt(jnp.maximum(squares - mean * mean, 0.0) + eps)
    qkv_copy.wait()
    mixed = jnp.zeros((rows, qkv.shape[1]), jnp.float32)
    for span in spans:
        centre = tokens[:, span].astype(jnp.float32) - mean
        normed = (centre * scale * gain_ref[:, span].astype(jnp.float32)).astype(jnp.bfloat16)
        mixed = mixed + dot(normed, qkv[span, :])
    head = norm_ref.shape[1]
    queries = head_norm(mixed[:, :head], norm_ref[0:1, :])
    keys = head_norm(mixed[:, head : 2 * head], norm_ref[1:2, :])
    values = mixed[:, 2 * head :].astype(jnp.bfloat16)
    lane = iota((rows, 128), 1)
    flags = x[:, TAIL:].astype(jnp.float32)
    flags = jnp.where((lane >= SRC_AT) & (lane < SRC_END), flags, 0.0)
    live = jnp.sum(flags, axis=1, keepdims=True) > 0.5
    flags = flags.astype(jnp.bfloat16)
    for at in range(0, rows, 128):
        here = slice(at, at + 128)
        first = min(max(at - 64, 0), rows - 256)
        near = slice(first, first + 256)
        same = dot(flags[here], flags[near], ((1,), (1,))) > 0.5
        scores = dot(queries[here], keys[near], ((1,), (1,))) * (1.0 / math.sqrt(head))
        scores = jnp.where(same, scores, -1e30)
        expo = jnp.exp(scores - jnp.max(scores, axis=1, keepdims=True))
        weights = (expo * (1.0 / jnp.sum(expo, axis=1, keepdims=True))).astype(jnp.bfloat16)
        attended = jnp.where(live[here], dot(weights, values[near]), 0.0)
        out_ref[here, :] = attended.astype(jnp.bfloat16)


def embed_kernel(x_ref, tile_ref, early_ref, late_ref, half_hbm, out_ref, half_ref, sem):
    copy = pltpu.make_async_copy(half_hbm, half_ref, sem.at[0])
    copy.start()
    for t in range(2 + late_ref.shape[0]):
        span = slice(t * TILE, (t + 1) * TILE)
        tile = (tile_ref[0, :TAIL], early_ref[0, :TAIL])[t] if t < 2 else late_ref[t - 2, :TAIL]
        out_ref[:, span] = dot(x_ref[:, :TAIL], tile)
    copy.wait()


def section_kernel(
    part_ref, x_ref, attended_ref, tile_ref, early_ref, late_ref, mine_ref, other_ref, out_hbm, weight, out, sems
):
    half = mine_ref.shape[0]
    last = x_ref.shape[1] - TAIL
    core = lax.axis_index("dp") % 2
    weight[pl.ds(pl.multiple_of(last + core * half, half), half), :] = mine_ref[...]
    weight[pl.ds(pl.multiple_of(last + (1 - core) * half, half), half), :] = other_ref[...]
    both = jnp.concatenate([x_ref[:, TAIL:], attended_ref[...]], axis=1)
    results = []
    for t in range(out.shape[1] // TILE):
        span = slice(t * TILE, (t + 1) * TILE)
        tile = (tile_ref[0, TAIL:], early_ref[0, TAIL:])[t] if t < 2 else late_ref[t - 2, TAIL:]
        weight[:last, span] = tile
        out[:, span] = (part_ref[:, span] + dot(both, weight[:, span])).astype(jnp.bfloat16)
        columns = pl.ds(t * TILE, TILE)
        result = pltpu.make_async_copy(out.at[:, columns], out_hbm.at[0, :, columns], sems.at[t])
        result.start()
        results.append(result)
    for result in results:
        result.wait()


VMEM = pl.BlockSpec(memory_space=pltpu.VMEM)
HBM = pl.BlockSpec(memory_space=pltpu.HBM)


def bf16(*shape):
    return jax.ShapeDtypeStruct(shape, jnp.bfloat16)


def call(kernel, out, in_specs, out_specs, scratch, limit, flops, aliases={}):
    return pl.pallas_call(
        kernel,
        out_shape=out,
        in_specs=in_specs,
        out_specs=out_specs,
        scratch_shapes=scratch,
        input_output_aliases=aliases,
        compiler_params=pltpu.CompilerParams(vmem_limit_bytes=limit * MIB),
        cost_estimate=pl.CostEstimate(flops=flops, bytes_accessed=MIB, transcendentals=0),
    )


def shards(
    patches,
    image_shape,
    keep_list,
    kept_count,
    dest_seq,
    embed_weight,
    pos_rows,
    pos_cols,
    ln_gain,
    qkv_weight,
    norm_gains,
    out_weight,
):
    groups = lax.axis_size("dp")
    segments = lax.axis_size("segment")
    images, patch_max, patch_width = patches.shape[1:]
    kept_max = keep_list.shape[2]
    seq_len = images * kept_max
    width = embed_weight.shape[1]
    head = out_weight.shape[1]
    tiles = width // TILE
    parts = 4
    onward = [(source, (source + 1) % segments) for source in range(segments)]
    pairs = [(source, source ^ 1) for source in range(groups)]
    dma = pltpu.SemaphoreType.DMA
    token = jax.ShapeDtypeStruct((8, 128), jnp.float32)

    packed, half, after_pack = call(
        pack_kernel,
        [bf16(groups, kept_max, LANES), bf16(head // 2, width), token],
        [HBM] * 6,
        [VMEM, HBM, VMEM],
        [
            pltpu.SMEM((2, images), jnp.int32),
            pltpu.SMEM((1, images), jnp.int32),
            pltpu.SMEM((1, images), jnp.int32),
            pltpu.VMEM((images, kept_max), jnp.int32),
            pltpu.VMEM((images, patch_max, patch_width), jnp.bfloat16),
            pltpu.VMEM((head // 2, width), jnp.bfloat16),
            dma((6,)),
            dma((parts,)),
        ],
        60,
        2 * images * kept_max * patch_max * LANES,
    )(image_shape[0].T, kept_count, dest_seq, keep_list[0], patches[0], out_weight[0])
    received = lax.all_to_all(packed, "dp", split_axis=0, concat_axis=0, tiled=True)

    half = lax.ppermute(half, "segment", onward)
    tail = jnp.concatenate(
        [
            embed_weight[LANES - 64 :],
            pos_rows,
            pos_cols,
            jnp.zeros((LANES - patch_width - 16, width), jnp.bfloat16),
        ],
        axis=0,
    )
    weights, tile = call(
        weight_kernel,
        [bf16(STORE, TILE), bf16(1, LANES, TILE)],
        [HBM] + [VMEM] * 3,
        [HBM, VMEM],
        [dma((2 * tiles + 3,))],
        20,
        MIB,
    )(after_pack, embed_weight, tail, qkv_weight[0])
    x, early = call(
        compact_kernel,
        [bf16(seq_len, LANES), bf16(1, LANES, TILE)],
        [HBM, VMEM],
        [VMEM] * 2,
        [dma((1,))],
        16,
        2 * seq_len * groups * kept_max * LANES,
    )(weights, received)
    next_x = lax.ppermute(x, "segment", onward)
    attended, late, after_attend = call(
        attend_kernel,
        [bf16(seq_len, head), bf16(tiles - 2, LANES, TILE), token],
        [VMEM] * 5 + [HBM],
        [VMEM] * 3,
        [
            pltpu.VMEM((seq_len, width), jnp.bfloat16),
            pltpu.VMEM((width, 3 * head), jnp.bfloat16),
            dma((tiles - 2,)),
            dma((1,)),
        ],
        34,
        2 * seq_len * width * (LANES + 3 * head),
    )(x, ln_gain, norm_gains[0], tile, early, weights)
    next_attended = lax.ppermute(attended, "segment", onward)
    half = call(hand_on_kernel, bf16(head // 2, width), [HBM, HBM], HBM, [], 4, MIB, {1: 0})(
        after_attend, half
    )
    other = lax.ppermute(half, "dp", pairs)

    part, half = call(
        embed_kernel,
        [jax.ShapeDtypeStruct((seq_len, width), jnp.float32), bf16(head // 2, width)],
        [VMEM] * 4 + [HBM],
        [VMEM] * 2,
        [dma((1,))],
        16,
        2 * seq_len * width * LANES,
    )(next_x, tile, early, late, half)
    return call(
        section_kernel,
        bf16(1, seq_len, width),
        [VMEM] * 8,
        HBM,
        [
            pltpu.VMEM((LANES - TAIL + head, width), jnp.bfloat16),
            pltpu.VMEM((seq_len, width), jnp.bfloat16),
            dma((tiles,)),
        ],
        20,
        2 * seq_len * width * head,
    )(part, next_x, next_attended, tile, early, late, half, other)


def solution(mesh):
    return jax.shard_map(
        shards,
        mesh=mesh,
        in_specs=(
            P("segment", "dp", None, None),
            P("segment", "dp", None),
            P("segment", "dp", None),
            P("segment", "dp"),
            P("segment", "dp"),
            P(),
            P(),
            P(),
            P("segment", None),
            P("segment", None, None),
            P("segment", None, None),
            P("segment", None, None),
        ),
        out_specs=P("segment", "dp", None),
        check_vma=False,
    )
```

```python
import math

import jax
import jax.numpy as jnp
from jax import lax
from jax.experimental import pallas as pl
from jax.experimental.pallas import tpu as pltpu
from jax.sharding import PartitionSpec as P

eps = 1e-06
LANES = 640
TAIL = 512
ROW_AT = 588 - TAIL
COL_AT = 596 - TAIL
SRC_AT = 604 - TAIL
SRC_END = 636 - TAIL
SIDE_MIN = 6
SIDE_MAX = 8
TILE = 1024
STORE = 20480
MIB = 1 << 20


def iota(shape, axis):
    return lax.broadcasted_iota(jnp.int32, shape, axis)


def dot(a, b, dims=((1,), (0,))):
    return lax.dot_general(a, b, (dims, ((), ())), preferred_element_type=jnp.float32)


def as_bf16(mask):
    return mask.astype(jnp.float32).astype(jnp.bfloat16)


def pack_kernel(
    shape_hbm, count_hbm, dest_hbm, keep_hbm, patches_hbm, weight_hbm, out_ref, half_ref, token_ref,
    shape, count, dest, keep, patches, sems, patch_sems,
):
    images, patch_max, _ = patches.shape
    kept_max = keep.shape[1]
    parts = patch_sems.shape[0]
    step = images // parts
    small = [
        pltpu.make_async_copy(source, target, sems.at[n])
        for n, (source, target) in enumerate(
            ((shape_hbm, shape), (count_hbm, count), (dest_hbm, dest), (keep_hbm, keep))
        )
    ]
    large = [
        pltpu.make_async_copy(
            patches_hbm.at[pl.ds(n * step, step)], patches.at[pl.ds(n * step, step)], patch_sems.at[n]
        )
        for n in range(parts)
    ]
    for copy in small + large:
        copy.start()
    device = lax.axis_index("dp")
    share = half_ref.shape[0]
    half = pltpu.make_async_copy(
        weight_hbm.at[pl.ds(pl.multiple_of(device % 2 * share, share), share)], half_ref, sems.at[4]
    )
    half.start()
    out_ref[...] = jnp.zeros_like(out_ref)
    token_ref[...] = jnp.zeros_like(token_ref)
    number = iota((patch_max, 128), 0)
    lane = iota((patch_max, 128), 1)
    source = lane == SRC_AT + device
    flags = {}
    for width in range(SIDE_MIN, SIDE_MAX + 1):
        row = jnp.zeros_like(number)
        for k in range(1, SIDE_MAX):
            row = row + (number >= k * width).astype(jnp.int32)
        col = number - row * width
        flags[width] = ((lane == ROW_AT + row) | (lane == COL_AT + col) | source).astype(jnp.float32)
    for copy in small:
        copy.wait()
    for g in range(images):
        if g % step == 0:
            large[g // step].wait()
        width = shape[1, g]
        own = flags[SIDE_MAX]
        for side in range(SIDE_MIN, SIDE_MAX):
            own = jnp.where(width == side, flags[side], own)
        picked = (iota((patch_max, kept_max), 0) == keep[g : g + 1, :]) & (
            iota((patch_max, kept_max), 1) < count[0, g]
        )
        picked = as_bf16(picked)
        there = dest[0, g]
        body = dot(picked, patches[g, :, :TAIL], ((0,), (0,)))
        out_ref[there, :, :TAIL] = body.astype(jnp.bfloat16)
        last = jnp.concatenate([patches[g, :, TAIL:], own.astype(jnp.bfloat16)[:, ROW_AT:]], axis=1)
        out_ref[there, :, TAIL:] = dot(picked, last, ((0,), (0,))).astype(jnp.bfloat16)
    half.wait()


def compact_kernel(weights_hbm, recv_ref, out_ref, early_ref, sems):
    (early,) = tile_copies(weights_hbm, 1, early_ref, sems)
    early.start()
    sources, kept_max, lanes = recv_ref.shape
    total = sources * kept_max
    blocks = total // 128
    seq_len = out_ref.shape[0]
    received = recv_ref[...].reshape(total, lanes)
    at = iota((8, 128), 1)
    select = as_bf16((at >= SRC_AT) & (at < SRC_END))
    live = dot(select, received[:, TAIL:], ((1,), (1,)))
    group = iota((8, 128), 0)
    packed = jnp.zeros((8, 128), jnp.float32)
    for b in range(blocks):
        packed = jnp.where(group == b, live[:, b * 128 : (b + 1) * 128], packed)
    before = as_bf16(iota((128, 128), 0) < iota((128, 128), 1))
    within = dot(packed.astype(jnp.bfloat16), before)
    sums = jnp.sum(packed, axis=1, keepdims=True)
    base = jnp.zeros((8, 1), jnp.float32)
    for b in range(blocks - 1):
        base = base + jnp.where(iota((8, 1), 0) > b, sums[b : b + 1, :], 0.0)
    place = jnp.where(packed > 0.5, within + base, -1.0).astype(jnp.int32)
    slot = iota((seq_len, 128), 0)
    hot = jnp.concatenate([as_bf16(slot == place[b : b + 1, :]) for b in range(blocks)], axis=1)
    out_ref[...] = dot(hot, received).astype(jnp.bfloat16)
    early.wait()


def lane_sums(values, sums):
    for at in range(0, values.shape[1], 128):
        sums = sums + values[:, at : at + 128]
    return sums


def head_norm(values, gain):
    centre = values - jnp.mean(values, axis=-1, keepdims=True)
    spread = jnp.mean(centre * centre, axis=-1, keepdims=True)
    return (centre * lax.rsqrt(spread + eps) * gain).astype(jnp.bfloat16)


def weight_kernel(token_hbm, embed_ref, tail_ref, qkv_ref, out_hbm, tile_ref, sems):
    tail = tail_ref.shape[0]
    depth = LANES - tail
    tiles = embed_ref.shape[1] // TILE
    copies = []
    for t in range(tiles):
        columns = pl.ds(t * TILE, TILE)
        for source, first, rows in ((embed_ref, t * LANES, depth), (tail_ref, t * LANES + depth, tail)):
            copies.append(
                pltpu.make_async_copy(
                    source.at[pl.ds(0, rows), columns], out_hbm.at[pl.ds(first, rows)], sems.at[len(copies)]
                )
            )
    columns = pl.ds(0, TILE)
    for source, first, rows in ((embed_ref, 0, depth), (tail_ref, depth, tail)):
        copies.append(
            pltpu.make_async_copy(
                source.at[pl.ds(0, rows), columns],
                tile_ref.at[0, pl.ds(first, rows)],
                sems.at[len(copies)],
            )
        )
    copies.append(
        pltpu.make_async_copy(qkv_ref, qkv_part(out_hbm, tiles * LANES, qkv_ref), sems.at[len(copies)])
    )
    for copy in copies:
        copy.start()
    for copy in copies:
        copy.wait()


def qkv_part(weights, first, qkv):
    return weights.at[pl.ds(first, qkv.shape[0]), pl.ds(0, qkv.shape[1])]


def tile_copies(weights_hbm, first, embed, sems):
    tiles, lanes, _ = embed.shape
    return [
        pltpu.make_async_copy(weights_hbm.at[pl.ds((first + t) * lanes, lanes)], embed.at[t], sems.at[t])
        for t in range(tiles)
    ]


def hand_on_kernel(token_hbm, half_hbm, same_half_hbm):
    pass


def attend_kernel(
    x_ref, gain_ref, norm_ref, tile_ref, early_ref, weights_hbm, out_ref, late_ref, token_ref,
    tokens, qkv, sems, qkv_sem,
):
    late, lanes, _ = late_ref.shape
    copies = tile_copies(weights_hbm, 2, late_ref, sems)
    qkv_copy = pltpu.make_async_copy(qkv_part(weights_hbm, (2 + late) * lanes, qkv), qkv, qkv_sem.at[0])
    width = (2 + late) * TILE
    copies[0].start()
    copies[1].start()
    token_ref[...] = jnp.zeros_like(token_ref)
    x = x_ref[...]
    rows = x.shape[0]
    spans = [slice(at, at + TILE) for at in range(0, width, TILE)]
    total = jnp.zeros((rows, 128), jnp.float32)
    squares = jnp.zeros((rows, 128), jnp.float32)
    for t, span in enumerate(spans):
        if t == 1:
            copies[2].start()
            copies[3].start()
        if t == 2:
            copies[0].wait()
            copies[1].wait()
            qkv_copy.start()
        if t == 4:
            copies[2].wait()
            copies[3].wait()
        tile = (tile_ref[0], early_ref[0])[t] if t < 2 else late_ref[t - 2]
        part = dot(x, tile).astype(jnp.bfloat16)
        tokens[:, span] = part
        part = part.astype(jnp.float32)
        total = lane_sums(part, total)
        squares = lane_sums(part * part, squares)
    mean = jnp.sum(total, axis=1, keepdims=True) / width
    squares = jnp.sum(squares, axis=1, keepdims=True) / width
    scale = lax.rsqrt(jnp.maximum(squares - mean * mean, 0.0) + eps)
    qkv_copy.wait()
    mixed = jnp.zeros((rows, qkv.shape[1]), jnp.float32)
    for span in spans:
        centre = tokens[:, span].astype(jnp.float32) - mean
        normed = (centre * scale * gain_ref[:, span].astype(jnp.float32)).astype(jnp.bfloat16)
        mixed = mixed + dot(normed, qkv[span, :])
    head = norm_ref.shape[1]
    queries = head_norm(mixed[:, :head], norm_ref[0:1, :])
    keys = head_norm(mixed[:, head : 2 * head], norm_ref[1:2, :])
    values = mixed[:, 2 * head :].astype(jnp.bfloat16)
    lane = iota((rows, 128), 1)
    flags = x[:, TAIL:].astype(jnp.float32)
    flags = jnp.where((lane >= SRC_AT) & (lane < SRC_END), flags, 0.0)
    live = jnp.sum(flags, axis=1, keepdims=True) > 0.5
    flags = flags.astype(jnp.bfloat16)
    for at in range(0, rows, 128):
        here = slice(at, at + 128)
        first = min(max(at - 64, 0), rows - 256)
        near = slice(first, first + 256)
        same = dot(flags[here], flags[near], ((1,), (1,))) > 0.5
        scores = dot(queries[here], keys[near], ((1,), (1,))) * (1.0 / math.sqrt(head))
        scores = jnp.where(same, scores, -1e30)
        expo = jnp.exp(scores - jnp.max(scores, axis=1, keepdims=True))
        weights = (expo * (1.0 / jnp.sum(expo, axis=1, keepdims=True))).astype(jnp.bfloat16)
        attended = jnp.where(live[here], dot(weights, values[near]), 0.0)
        out_ref[here, :] = attended.astype(jnp.bfloat16)


def embed_kernel(x_ref, tile_ref, early_ref, late_ref, half_hbm, out_ref, half_ref, sem):
    copy = pltpu.make_async_copy(half_hbm, half_ref, sem.at[0])
    copy.start()
    for t in range(2 + late_ref.shape[0]):
        span = slice(t * TILE, (t + 1) * TILE)
        tile = (tile_ref[0, :TAIL], early_ref[0, :TAIL])[t] if t < 2 else late_ref[t - 2, :TAIL]
        out_ref[:, span] = dot(x_ref[:, :TAIL], tile)
    copy.wait()


def section_kernel(
    part_ref, x_ref, attended_ref, tile_ref, early_ref, late_ref, mine_ref, other_ref, out_hbm, weight, out, sems
):
    half = mine_ref.shape[0]
    last = x_ref.shape[1] - TAIL
    core = lax.axis_index("dp") % 2
    weight[pl.ds(pl.multiple_of(last + core * half, half), half), :] = mine_ref[...]
    weight[pl.ds(pl.multiple_of(last + (1 - core) * half, half), half), :] = other_ref[...]
    both = jnp.concatenate([x_ref[:, TAIL:], attended_ref[...]], axis=1)
    results = []
    for t in range(out.shape[1] // TILE):
        span = slice(t * TILE, (t + 1) * TILE)
        tile = (tile_ref[0, TAIL:], early_ref[0, TAIL:])[t] if t < 2 else late_ref[t - 2, TAIL:]
        weight[:last, span] = tile
        out[:, span] = (part_ref[:, span] + dot(both, weight[:, span])).astype(jnp.bfloat16)
        columns = pl.ds(t * TILE, TILE)
        result = pltpu.make_async_copy(out.at[:, columns], out_hbm.at[0, :, columns], sems.at[t])
        result.start()
        results.append(result)
    for result in results:
        result.wait()


VMEM = pl.BlockSpec(memory_space=pltpu.VMEM)
HBM = pl.BlockSpec(memory_space=pltpu.HBM)


def bf16(*shape):
    return jax.ShapeDtypeStruct(shape, jnp.bfloat16)


def call(kernel, out, in_specs, out_specs, scratch, limit, flops, aliases={}):
    return pl.pallas_call(
        kernel,
        out_shape=out,
        in_specs=in_specs,
        out_specs=out_specs,
        scratch_shapes=scratch,
        input_output_aliases=aliases,
        compiler_params=pltpu.CompilerParams(vmem_limit_bytes=limit * MIB),
        cost_estimate=pl.CostEstimate(flops=flops, bytes_accessed=MIB, transcendentals=0),
    )


def shards(
    patches,
    image_shape,
    keep_list,
    kept_count,
    dest_seq,
    embed_weight,
    pos_rows,
    pos_cols,
    ln_gain,
    qkv_weight,
    norm_gains,
    out_weight,
):
    groups = lax.axis_size("dp")
    segments = lax.axis_size("segment")
    images, patch_max, patch_width = patches.shape[1:]
    kept_max = keep_list.shape[2]
    seq_len = images * kept_max
    width = embed_weight.shape[1]
    head = out_weight.shape[1]
    tiles = width // TILE
    parts = 1
    onward = [(source, (source + 1) % segments) for source in range(segments)]
    pairs = [(source, source ^ 1) for source in range(groups)]
    dma = pltpu.SemaphoreType.DMA
    token = jax.ShapeDtypeStruct((8, 128), jnp.float32)

    packed, half, after_pack = call(
        pack_kernel,
        [bf16(groups, kept_max, LANES), bf16(head // 2, width), token],
        [HBM] * 6,
        [VMEM] * 3,
        [
            pltpu.SMEM((2, images), jnp.int32),
            pltpu.SMEM((1, images), jnp.int32),
            pltpu.SMEM((1, images), jnp.int32),
            pltpu.VMEM((images, kept_max), jnp.int32),
            pltpu.VMEM((images, patch_max, patch_width), jnp.bfloat16),
            dma((5,)),
            dma((parts,)),
        ],
        60,
        2 * images * kept_max * patch_max * LANES,
    )(image_shape[0].T, kept_count, dest_seq, keep_list[0], patches[0], out_weight[0])
    received = lax.all_to_all(packed, "dp", split_axis=0, concat_axis=0, tiled=True)

    half = lax.ppermute(half, "segment", onward)
    tail = jnp.concatenate(
        [
            embed_weight[LANES - 64 :],
            pos_rows,
            pos_cols,
            jnp.zeros((LANES - patch_width - 16, width), jnp.bfloat16),
        ],
        axis=0,
    )
    weights, tile = call(
        weight_kernel,
        [bf16(STORE, TILE), bf16(1, LANES, TILE)],
        [HBM] + [VMEM] * 3,
        [HBM, VMEM],
        [dma((2 * tiles + 3,))],
        20,
        MIB,
    )(after_pack, embed_weight, tail, qkv_weight[0])
    x, early = call(
        compact_kernel,
        [bf16(seq_len, LANES), bf16(1, LANES, TILE)],
        [HBM, VMEM],
        [VMEM] * 2,
        [dma((1,))],
        16,
        2 * seq_len * groups * kept_max * LANES,
    )(weights, received)
    next_x = lax.ppermute(x, "segment", onward)
    attended, late, after_attend = call(
        attend_kernel,
        [bf16(seq_len, head), bf16(tiles - 2, LANES, TILE), token],
        [VMEM] * 5 + [HBM],
        [VMEM] * 3,
        [
            pltpu.VMEM((seq_len, width), jnp.bfloat16),
            pltpu.VMEM((width, 3 * head), jnp.bfloat16),
            dma((tiles - 2,)),
            dma((1,)),
        ],
        34,
        2 * seq_len * width * (LANES + 3 * head),
    )(x, ln_gain, norm_gains[0], tile, early, weights)
    next_attended = lax.ppermute(attended, "segment", onward)
    half = call(hand_on_kernel, bf16(head // 2, width), [HBM, HBM], HBM, [], 4, MIB, {1: 0})(
        after_attend, half
    )
    other = lax.ppermute(half, "dp", pairs)

    part, half = call(
        embed_kernel,
        [jax.ShapeDtypeStruct((seq_len, width), jnp.float32), bf16(head // 2, width)],
        [VMEM] * 4 + [HBM],
        [VMEM] * 2,
        [dma((1,))],
        16,
        2 * seq_len * width * LANES,
    )(next_x, tile, early, late, half)
    return call(
        section_kernel,
        bf16(1, seq_len, width),
        [VMEM] * 8,
        HBM,
        [
            pltpu.VMEM((LANES - TAIL + head, width), jnp.bfloat16),
            pltpu.VMEM((seq_len, width), jnp.bfloat16),
            dma((tiles,)),
        ],
        20,
        2 * seq_len * width * head,
    )(part, next_x, next_attended, tile, early, late, half, other)


def solution(mesh):
    return jax.shard_map(
        shards,
        mesh=mesh,
        in_specs=(
            P("segment", "dp", None, None),
            P("segment", "dp", None),
            P("segment", "dp", None),
            P("segment", "dp"),
            P("segment", "dp"),
            P(),
            P(),
            P(),
            P("segment", None),
            P("segment", None, None),
            P("segment", None, None),
            P("segment", None, None),
        ),
        out_specs=P("segment", "dp", None),
        check_vma=False,
    )
```

```python
import math

import jax
import jax.numpy as jnp
from jax import lax
from jax.experimental import pallas as pl
from jax.experimental.pallas import tpu as pltpu
from jax.sharding import PartitionSpec as P

eps = 1e-06
LANES = 640
TAIL = 512
ROW_AT = 588 - TAIL
COL_AT = 596 - TAIL
SRC_AT = 604 - TAIL
SRC_END = 636 - TAIL
SIDE_MIN = 6
SIDE_MAX = 8
TILE = 1024
STORE = 20480
MIB = 1 << 20


def iota(shape, axis):
    return lax.broadcasted_iota(jnp.int32, shape, axis)


def dot(a, b, dims=((1,), (0,))):
    return lax.dot_general(a, b, (dims, ((), ())), preferred_element_type=jnp.float32)


def as_bf16(mask):
    return mask.astype(jnp.float32).astype(jnp.bfloat16)


def pack_kernel(
    shape_hbm, count_hbm, dest_hbm, keep_hbm, patches_hbm, weight_hbm, out_ref, half_ref, token_ref,
    shape, count, dest, keep, patches, sems, patch_sems,
):
    images, patch_max, _ = patches.shape
    kept_max = keep.shape[1]
    parts = patch_sems.shape[0]
    step = images // parts
    small = [
        pltpu.make_async_copy(source, target, sems.at[n])
        for n, (source, target) in enumerate(
            ((shape_hbm, shape), (count_hbm, count), (dest_hbm, dest), (keep_hbm, keep))
        )
    ]
    large = [
        pltpu.make_async_copy(
            patches_hbm.at[pl.ds(n * step, step)], patches.at[pl.ds(n * step, step)], patch_sems.at[n]
        )
        for n in range(parts)
    ]
    for copy in small + large:
        copy.start()
    device = lax.axis_index("dp")
    share = half_ref.shape[0]
    half = pltpu.make_async_copy(
        weight_hbm.at[pl.ds(pl.multiple_of(device % 2 * share, share), share)], half_ref, sems.at[4]
    )
    half.start()
    out_ref[...] = jnp.zeros_like(out_ref)
    token_ref[...] = jnp.zeros_like(token_ref)
    number = iota((patch_max, 128), 0)
    lane = iota((patch_max, 128), 1)
    source = lane == SRC_AT + device
    flags = {}
    for width in range(SIDE_MIN, SIDE_MAX + 1):
        row = jnp.zeros_like(number)
        for k in range(1, SIDE_MAX):
            row = row + (number >= k * width).astype(jnp.int32)
        col = number - row * width
        flags[width] = ((lane == ROW_AT + row) | (lane == COL_AT + col) | source).astype(jnp.float32)
    for copy in small:
        copy.wait()
    for g in range(images):
        if g % step == 0:
            large[g // step].wait()
        width = shape[1, g]
        own = flags[SIDE_MAX]
        for side in range(SIDE_MIN, SIDE_MAX):
            own = jnp.where(width == side, flags[side], own)
        picked = (iota((patch_max, kept_max), 0) == keep[g : g + 1, :]) & (
            iota((patch_max, kept_max), 1) < count[0, g]
        )
        picked = as_bf16(picked)
        there = dest[0, g]
        body = dot(picked, patches[g, :, :TAIL], ((0,), (0,)))
        out_ref[there, :, :TAIL] = body.astype(jnp.bfloat16)
        last = jnp.concatenate([patches[g, :, TAIL:], own.astype(jnp.bfloat16)[:, ROW_AT:]], axis=1)
        out_ref[there, :, TAIL:] = dot(picked, last, ((0,), (0,))).astype(jnp.bfloat16)
    half.wait()


def compact_kernel(weights_hbm, recv_ref, out_ref, early_ref, sems):
    (early,) = tile_copies(weights_hbm, 1, early_ref, sems)
    early.start()
    sources, kept_max, lanes = recv_ref.shape
    total = sources * kept_max
    blocks = total // 128
    seq_len = out_ref.shape[0]
    received = recv_ref[...].reshape(total, lanes)
    at = iota((8, 128), 1)
    select = as_bf16((at >= SRC_AT) & (at < SRC_END))
    live = dot(select, received[:, TAIL:], ((1,), (1,)))
    group = iota((8, 128), 0)
    packed = jnp.zeros((8, 128), jnp.float32)
    for b in range(blocks):
        packed = jnp.where(group == b, live[:, b * 128 : (b + 1) * 128], packed)
    before = as_bf16(iota((128, 128), 0) < iota((128, 128), 1))
    within = dot(packed.astype(jnp.bfloat16), before)
    sums = jnp.sum(packed, axis=1, keepdims=True)
    base = jnp.zeros((8, 1), jnp.float32)
    for b in range(blocks - 1):
        base = base + jnp.where(iota((8, 1), 0) > b, sums[b : b + 1, :], 0.0)
    place = jnp.where(packed > 0.5, within + base, -1.0).astype(jnp.int32)
    slot = iota((seq_len, 128), 0)
    hot = jnp.concatenate([as_bf16(slot == place[b : b + 1, :]) for b in range(blocks)], axis=1)
    out_ref[...] = dot(hot, received).astype(jnp.bfloat16)
    early.wait()


def lane_sums(values, sums):
    for at in range(0, values.shape[1], 128):
        sums = sums + values[:, at : at + 128]
    return sums


def head_norm(values, gain):
    centre = values - jnp.mean(values, axis=-1, keepdims=True)
    spread = jnp.mean(centre * centre, axis=-1, keepdims=True)
    return (centre * lax.rsqrt(spread + eps) * gain).astype(jnp.bfloat16)


def weight_kernel(token_hbm, embed_ref, tail_ref, qkv_ref, out_hbm, tile_ref, sems):
    tail = tail_ref.shape[0]
    depth = LANES - tail
    tiles = embed_ref.shape[1] // TILE
    copies = []
    for t in range(tiles):
        columns = pl.ds(t * TILE, TILE)
        for source, first, rows in ((embed_ref, t * LANES, depth), (tail_ref, t * LANES + depth, tail)):
            copies.append(
                pltpu.make_async_copy(
                    source.at[pl.ds(0, rows), columns], out_hbm.at[pl.ds(first, rows)], sems.at[len(copies)]
                )
            )
    columns = pl.ds(0, TILE)
    for source, first, rows in ((embed_ref, 0, depth), (tail_ref, depth, tail)):
        copies.append(
            pltpu.make_async_copy(
                source.at[pl.ds(0, rows), columns],
                tile_ref.at[0, pl.ds(first, rows)],
                sems.at[len(copies)],
            )
        )
    copies.append(
        pltpu.make_async_copy(qkv_ref, qkv_part(out_hbm, tiles * LANES, qkv_ref), sems.at[len(copies)])
    )
    for copy in copies:
        copy.start()
    for copy in copies:
        copy.wait()


def qkv_part(weights, first, qkv):
    return weights.at[pl.ds(first, qkv.shape[0]), pl.ds(0, qkv.shape[1])]


def tile_copies(weights_hbm, first, embed, sems):
    tiles, lanes, _ = embed.shape
    return [
        pltpu.make_async_copy(weights_hbm.at[pl.ds((first + t) * lanes, lanes)], embed.at[t], sems.at[t])
        for t in range(tiles)
    ]


def hand_on_kernel(token_hbm, half_hbm, same_half_hbm):
    pass


def attend_kernel(
    x_ref, gain_ref, norm_ref, tile_ref, early_ref, weights_hbm, out_ref, late_ref, token_ref,
    tokens, qkv, sems, qkv_sem,
):
    late, lanes, _ = late_ref.shape
    copies = tile_copies(weights_hbm, 2, late_ref, sems)
    qkv_copy = pltpu.make_async_copy(qkv_part(weights_hbm, (2 + late) * lanes, qkv), qkv, qkv_sem.at[0])
    width = (2 + late) * TILE
    copies[0].start()
    copies[1].start()
    token_ref[...] = jnp.zeros_like(token_ref)
    x = x_ref[...]
    rows = x.shape[0]
    spans = [slice(at, at + TILE) for at in range(0, width, TILE)]
    total = jnp.zeros((rows, 128), jnp.float32)
    squares = jnp.zeros((rows, 128), jnp.float32)
    for t, span in enumerate(spans):
        if t == 1:
            copies[2].start()
            copies[3].start()
        if t == 2:
            copies[0].wait()
            copies[1].wait()
            qkv_copy.start()
        if t == 4:
            copies[2].wait()
            copies[3].wait()
        tile = (tile_ref[0], early_ref[0])[t] if t < 2 else late_ref[t - 2]
        part = dot(x, tile).astype(jnp.bfloat16)
        tokens[:, span] = part
        part = part.astype(jnp.float32)
        total = lane_sums(part, total)
        squares = lane_sums(part * part, squares)
    mean = jnp.sum(total, axis=1, keepdims=True) / width
    squares = jnp.sum(squares, axis=1, keepdims=True) / width
    scale = lax.rsqrt(jnp.maximum(squares - mean * mean, 0.0) + eps)
    qkv_copy.wait()
    mixed = jnp.zeros((rows, qkv.shape[1]), jnp.float32)
    for span in spans:
        centre = tokens[:, span].astype(jnp.float32) - mean
        normed = (centre * scale * gain_ref[:, span].astype(jnp.float32)).astype(jnp.bfloat16)
        mixed = mixed + dot(normed, qkv[span, :])
    head = norm_ref.shape[1]
    queries = head_norm(mixed[:, :head], norm_ref[0:1, :])
    keys = head_norm(mixed[:, head : 2 * head], norm_ref[1:2, :])
    values = mixed[:, 2 * head :].astype(jnp.bfloat16)
    lane = iota((rows, 128), 1)
    flags = x[:, TAIL:].astype(jnp.float32)
    flags = jnp.where((lane >= SRC_AT) & (lane < SRC_END), flags, 0.0)
    live = jnp.sum(flags, axis=1, keepdims=True) > 0.5
    flags = flags.astype(jnp.bfloat16)
    for at in range(0, rows, 128):
        here = slice(at, at + 128)
        first = min(max(at - 64, 0), rows - 256)
        near = slice(first, first + 256)
        same = dot(flags[here], flags[near], ((1,), (1,))) > 0.5
        scores = dot(queries[here], keys[near], ((1,), (1,))) * (1.0 / math.sqrt(head))
        scores = jnp.where(same, scores, -1e30)
        expo = jnp.exp(scores - jnp.max(scores, axis=1, keepdims=True))
        weights = (expo * (1.0 / jnp.sum(expo, axis=1, keepdims=True))).astype(jnp.bfloat16)
        attended = jnp.where(live[here], dot(weights, values[near]), 0.0)
        out_ref[here, :] = attended.astype(jnp.bfloat16)


def join_kernel(tile_ref, early_ref, late_ref, half_hbm, out_ref, token_ref, half, sem):
    copy = pltpu.make_async_copy(half_hbm, half, sem.at[0])
    copy.start()
    token_ref[...] = jnp.zeros_like(token_ref)
    last = LANES - TAIL
    share = half.shape[0]
    core = lax.axis_index("dp") % 2
    for t in range(2 + late_ref.shape[0]):
        tile = (tile_ref[0, TAIL:], early_ref[0, TAIL:])[t] if t < 2 else late_ref[t - 2, TAIL:]
        out_ref[:last, t * TILE : (t + 1) * TILE] = tile
    out_ref[pl.ds(pl.multiple_of(last + (1 - core) * share, share), share), :] = jnp.zeros_like(half)
    copy.wait()
    out_ref[pl.ds(pl.multiple_of(last + core * share, share), share), :] = half[...]


def embed_kernel(token_hbm, x_ref, tile_ref, early_ref, late_ref, out_ref):
    for t in range(2 + late_ref.shape[0]):
        span = slice(t * TILE, (t + 1) * TILE)
        tile = (tile_ref[0, :TAIL], early_ref[0, :TAIL])[t] if t < 2 else late_ref[t - 2, :TAIL]
        out_ref[:, span] = dot(x_ref[:, :TAIL], tile)


def section_kernel(
    part_ref, x_ref, attended_ref, joined_ref, other_ref, out_hbm, weight_ref, out, sems
):
    share = other_ref.shape[0]
    core = lax.axis_index("dp") % 2
    first = weight_ref.shape[0] - (1 + core) * share
    weight_ref[pl.ds(pl.multiple_of(first, share), share), :] = other_ref[...]
    both = jnp.concatenate([x_ref[:, TAIL:], attended_ref[...]], axis=1)
    results = []
    for t in range(out.shape[1] // TILE):
        span = slice(t * TILE, (t + 1) * TILE)
        out[:, span] = (part_ref[:, span] + dot(both, weight_ref[:, span])).astype(jnp.bfloat16)
        columns = pl.ds(t * TILE, TILE)
        result = pltpu.make_async_copy(out.at[:, columns], out_hbm.at[0, :, columns], sems.at[t])
        result.start()
        results.append(result)
    for result in results:
        result.wait()


VMEM = pl.BlockSpec(memory_space=pltpu.VMEM)
HBM = pl.BlockSpec(memory_space=pltpu.HBM)


def bf16(*shape):
    return jax.ShapeDtypeStruct(shape, jnp.bfloat16)


def call(kernel, out, in_specs, out_specs, scratch, limit, flops, aliases={}):
    return pl.pallas_call(
        kernel,
        out_shape=out,
        in_specs=in_specs,
        out_specs=out_specs,
        scratch_shapes=scratch,
        input_output_aliases=aliases,
        compiler_params=pltpu.CompilerParams(vmem_limit_bytes=limit * MIB),
        cost_estimate=pl.CostEstimate(flops=flops, bytes_accessed=MIB, transcendentals=0),
    )


def shards(
    patches,
    image_shape,
    keep_list,
    kept_count,
    dest_seq,
    embed_weight,
    pos_rows,
    pos_cols,
    ln_gain,
    qkv_weight,
    norm_gains,
    out_weight,
):
    groups = lax.axis_size("dp")
    segments = lax.axis_size("segment")
    images, patch_max, patch_width = patches.shape[1:]
    kept_max = keep_list.shape[2]
    seq_len = images * kept_max
    width = embed_weight.shape[1]
    head = out_weight.shape[1]
    tiles = width // TILE
    parts = 1
    onward = [(source, (source + 1) % segments) for source in range(segments)]
    pairs = [(source, source ^ 1) for source in range(groups)]
    dma = pltpu.SemaphoreType.DMA
    token = jax.ShapeDtypeStruct((8, 128), jnp.float32)

    packed, half, after_pack = call(
        pack_kernel,
        [bf16(groups, kept_max, LANES), bf16(head // 2, width), token],
        [HBM] * 6,
        [VMEM] * 3,
        [
            pltpu.SMEM((2, images), jnp.int32),
            pltpu.SMEM((1, images), jnp.int32),
            pltpu.SMEM((1, images), jnp.int32),
            pltpu.VMEM((images, kept_max), jnp.int32),
            pltpu.VMEM((images, patch_max, patch_width), jnp.bfloat16),
            dma((5,)),
            dma((parts,)),
        ],
        60,
        2 * images * kept_max * patch_max * LANES,
    )(image_shape[0].T, kept_count, dest_seq, keep_list[0], patches[0], out_weight[0])
    received = lax.all_to_all(packed, "dp", split_axis=0, concat_axis=0, tiled=True)

    half = lax.ppermute(half, "segment", onward)
    tail = jnp.concatenate(
        [
            embed_weight[LANES - 64 :],
            pos_rows,
            pos_cols,
            jnp.zeros((LANES - patch_width - 16, width), jnp.bfloat16),
        ],
        axis=0,
    )
    weights, tile = call(
        weight_kernel,
        [bf16(STORE, TILE), bf16(1, LANES, TILE)],
        [HBM] + [VMEM] * 3,
        [HBM, VMEM],
        [dma((2 * tiles + 3,))],
        20,
        MIB,
    )(after_pack, embed_weight, tail, qkv_weight[0])
    x, early = call(
        compact_kernel,
        [bf16(seq_len, LANES), bf16(1, LANES, TILE)],
        [HBM, VMEM],
        [VMEM] * 2,
        [dma((1,))],
        16,
        2 * seq_len * groups * kept_max * LANES,
    )(weights, received)
    next_x = lax.ppermute(x, "segment", onward)
    attended, late, after_attend = call(
        attend_kernel,
        [bf16(seq_len, head), bf16(tiles - 2, LANES, TILE), token],
        [VMEM] * 5 + [HBM],
        [VMEM] * 3,
        [
            pltpu.VMEM((seq_len, width), jnp.bfloat16),
            pltpu.VMEM((width, 3 * head), jnp.bfloat16),
            dma((tiles - 2,)),
            dma((1,)),
        ],
        34,
        2 * seq_len * width * (LANES + 3 * head),
    )(x, ln_gain, norm_gains[0], tile, early, weights)
    next_attended = lax.ppermute(attended, "segment", onward)
    half = call(hand_on_kernel, bf16(head // 2, width), [HBM, HBM], HBM, [], 4, MIB, {1: 0})(
        after_attend, half
    )
    other = lax.ppermute(half, "dp", pairs)

    joined, after_join = call(
        join_kernel,
        [bf16(LANES - TAIL + head, width), token],
        [VMEM] * 3 + [HBM],
        [VMEM] * 2,
        [pltpu.VMEM((head // 2, width), jnp.bfloat16), dma((1,))],
        12,
        MIB,
    )(tile, early, late, half)
    part = call(
        embed_kernel,
        jax.ShapeDtypeStruct((seq_len, width), jnp.float32),
        [HBM] + [VMEM] * 4,
        VMEM,
        [],
        16,
        2 * seq_len * width * LANES,
    )(after_join, next_x, tile, early, late)
    out, _ = call(
        section_kernel,
        [bf16(1, seq_len, width), bf16(LANES - TAIL + head, width)],
        [VMEM] * 5,
        [HBM, VMEM],
        [pltpu.VMEM((seq_len, width), jnp.bfloat16), dma((tiles,))],
        20,
        2 * seq_len * width * head,
        {3: 1},
    )(part, next_x, next_attended, joined, other)
    return out


def solution(mesh):
    return jax.shard_map(
        shards,
        mesh=mesh,
        in_specs=(
            P("segment", "dp", None, None),
            P("segment", "dp", None),
            P("segment", "dp", None),
            P("segment", "dp"),
            P("segment", "dp"),
            P(),
            P(),
            P(),
            P("segment", None),
            P("segment", None, None),
            P("segment", None, None),
            P("segment", None, None),
        ),
        out_specs=P("segment", "dp", None),
        check_vma=False,
    )
```
